512 devices in a mesh: ens: 4 (over y_hi, core), lat: 32 (over z, y_lo), lon: 4 (over x).
Axes of the slice: x: 4, y: 4 (y_hi: 2, y_lo: 2; y = y_hi * 2 + y_lo), z: 16, core: 2. Of those that a mesh axis runs over, the one named last changes fastest.
Arguments:
- state_field: bfloat16 [4, 256, 64, 512], P('ens', None, 'lat', 'lon'), may hold values from -6 to 6
- first_weight: bfloat16 [3, 256, 256], replicated, may hold values from -0.21875 to 0.21875
- second_weight: bfloat16 [3, 256, 256], replicated, may hold values from -0.21875 to 0.21875
- quadrature: float32 [64, 3, 12], P('lat'), may hold values from 0.05 to 0.4
- lat_offsets: int32 [64, 3, 12], P('lat'), may hold values from -1 to 1, as said below
- lon_offsets: int32 [64, 3, 12], P('lat'), may hold values from -4 to 4, as said below
- cotangent: bfloat16 [4, 256, 64, 512], P('ens', None, 'lat', 'lon'), may hold values from -6 to 6
Outputs:
- layer_output: bfloat16 [4, 256, 64, 512], P('ens', None, 'lat', 'lon')
- state_grad: bfloat16 [4, 256, 64, 512], P('ens', None, 'lat', 'lon')
- first_grad: float32 [3, 256, 256], replicated
- second_grad: float32 [3, 256, 256], replicated
The draws below stay inside these ranges and needn't reach their ends.
Inputs may be any that keep to these rules, and one draw needn't show every extreme that they name: `lat_offsets`: for every row and basis function the first three support points have latitude offsets 0, -1 and 1. `lon_offsets`: in a row p rows from the nearer pole the longitude offsets lie within plus or minus max(2, 4 - p), and the first three support points have offsets 0, minus that bound and that bound.
All inputs are finite; a program needn't handle non-finite values.
Results may differ from the reference program's by a relative error of at most 0.013.
Values may be sent and summed in bfloat16 or wider, within the bound.
A program may use at most 64 MiB of HBM per device.

```python
import math
from functools import partial
import jax
import jax.numpy as jnp
from jax import lax

CHANNELS = 256
BASIS = 3
SUPPORT = 12
LAT_REACH = 1
LON_REACH = 4
MEMBERS = 4
NLAT = 64
NLON = 512


def draw_lat_offsets(key, part):
    sub_key = jax.random.fold_in(key, 11)
    table_shape = (NLAT, BASIS, SUPPORT)
    values = jax.random.randint(sub_key, table_shape, -LAT_REACH, LAT_REACH + 1)
    slot_index = lax.broadcasted_iota(jnp.int32, table_shape, 2)
    values = jnp.where(slot_index == 0, 0, values)
    values = jnp.where(slot_index == 1, -LAT_REACH, values)
    values = jnp.where(slot_index == 2, LAT_REACH, values)
    return values.astype(jnp.int32)


def draw_lon_offsets(key, part):
    sub_key = jax.random.fold_in(key, 23)
    table_shape = (NLAT, BASIS, SUPPORT)
    row_index = lax.broadcasted_iota(jnp.int32, table_shape, 0)
    pole_distance = jnp.minimum(row_index, NLAT - 1 - row_index)
    reach_row = jnp.maximum(2, LON_REACH - pole_distance)
    raw_values = jax.random.randint(sub_key, table_shape, 0, 65536)
    values = raw_values % (2 * reach_row + 1) - reach_row
    slot_index = lax.broadcasted_iota(jnp.int32, table_shape, 2)
    values = jnp.where(slot_index == 0, 0, values)
    values = jnp.where(slot_index == 1, -reach_row, values)
    values = jnp.where(slot_index == 2, reach_row, values)
    return values.astype(jnp.int32)


def level_of(rng, extent, shards, least, largest):
    gain = 1.0
    for position, shards_of in shards:
        steps = jax.random.uniform(jax.random.fold_in(jax.random.fold_in(rng, 6), position), (shards_of,), jnp.float32, least / len(shards), largest / len(shards))
        gain = gain * jnp.repeat(jnp.exp(steps), extent[position] // shards_of).reshape((-1,) + (1,) * (len(extent) - 1 - position))
    return gain


def gaussian(stream_key, extent, scale, most, pieces=(), kind=jnp.bfloat16):
    values = scale * jax.random.normal(stream_key, extent, jnp.float32)
    if pieces:
        values = values * level_of(stream_key, extent, pieces, -0.22, 0.18)
    return jnp.clip(values, -most, most).astype(kind)


def setup_inputs(seed: int = 0) -> dict:
    seeds = jax.random.split(jax.random.key(seed), 8)
    state_field = gaussian(seeds[0], (MEMBERS, CHANNELS, NLAT, NLON), 1.0, 6.0, ((0, 4), (2, 32), (3, 4)))
    first_weight = gaussian(seeds[1], (BASIS, CHANNELS, CHANNELS), (CHANNELS * BASIS) ** -0.5, 0.21875)
    second_weight = gaussian(seeds[2], (BASIS, CHANNELS, CHANNELS), (CHANNELS * BASIS) ** -0.5, 0.21875)
    quadrature = jnp.clip(jnp.exp(math.log(0.4) - 2.0794415 * jax.random.uniform(seeds[3], (NLAT, BASIS, SUPPORT), jnp.float32) ** level_of(seeds[3], (NLAT, BASIS, SUPPORT), ((0, 32),), -0.2, 0.2)), 0.05, 0.4)
    lat_offsets = draw_lat_offsets(jax.random.fold_in(seeds[7], 71), 0)
    lon_offsets = draw_lon_offsets(jax.random.fold_in(seeds[7], 71), 0)
    cotangent = gaussian(seeds[6], (MEMBERS, CHANNELS, NLAT, NLON), 1.0, 6.0, ((0, 4), (2, 32), (3, 4)))
    return dict(state_field=state_field, first_weight=first_weight, second_weight=second_weight, quadrature=quadrature, lat_offsets=lat_offsets, lon_offsets=lon_offsets, cotangent=cotangent)


def coefficients(quadrature, lat_offsets, lon_offsets):
    lat_levels = jnp.arange(2 * LAT_REACH + 1, dtype=jnp.int32)
    lon_levels = jnp.arange(2 * LON_REACH + 1, dtype=jnp.int32)
    lat_onehot = (lat_offsets[..., None] + LAT_REACH == lat_levels).astype(jnp.float32)
    lon_onehot = (lon_offsets[..., None] + LON_REACH == lon_levels).astype(jnp.float32)
    stencil = jnp.einsum('rks,rksa,rksd->krad', quadrature, lat_onehot, lon_onehot, precision=lax.Precision.HIGHEST)
    return stencil.astype(jnp.bfloat16)

def spread(source, stencil):
    lat_taps = 2 * LAT_REACH + 1
    padded = jnp.pad(source, ((0, 0), (LAT_REACH, LAT_REACH), (0, 0)))

    def one_row(row_index):
        nearby = lax.dynamic_slice_in_dim(padded, row_index, lat_taps, 1)
        shifted = jnp.stack([jnp.roll(nearby, LON_REACH - offset, axis=2) for offset in range(2 * LON_REACH + 1)], axis=2)
        weights = lax.dynamic_index_in_dim(stencil, row_index, 1, keepdims=False)
        return jnp.einsum('cadj,kad->ckj', shifted, weights, precision=lax.Precision.HIGHEST)
    rows_out = lax.map(one_row, jnp.arange(NLAT, dtype=jnp.int32))
    return jnp.transpose(rows_out, (1, 2, 0, 3))

def mix_channels(weight, spreaded):
    return jnp.einsum('koc,ckij->oij', weight.astype(jnp.float32), spreaded.astype(jnp.float32), precision=lax.Precision.HIGHEST)

def unmix(weight, gradient):
    return jnp.einsum('koc,oij->ckij', weight.astype(jnp.float32), gradient.astype(jnp.float32), precision=lax.Precision.HIGHEST).astype(jnp.bfloat16)

def filter_term(gradient, spreaded):
    return jnp.einsum('oij,ckij->koc', gradient.astype(jnp.float32), spreaded.astype(jnp.float32), precision=lax.Precision.HIGHEST)

def reference(state_field, first_weight, second_weight, quadrature, lat_offsets, lon_offsets, cotangent):
    stencil = coefficients(quadrature, lat_offsets, lon_offsets).astype(jnp.float32)
    outputs = []
    state_grads = []
    first_sum = jnp.zeros((BASIS, CHANNELS, CHANNELS), jnp.float32)
    second_sum = jnp.zeros((BASIS, CHANNELS, CHANNELS), jnp.float32)
    for member in range(MEMBERS):
        source = state_field[member].astype(jnp.float32)
        first_spread = spread(source, stencil).astype(jnp.bfloat16)
        hidden = mix_channels(first_weight, first_spread)
        activation = jax.nn.gelu(hidden).astype(jnp.bfloat16)
        back_second = jax.vjp(partial(spread, stencil=stencil), activation.astype(jnp.float32))[1]
        second_spread = spread(activation.astype(jnp.float32), stencil).astype(jnp.bfloat16)
        outputs.append(mix_channels(second_weight, second_spread).astype(jnp.bfloat16))
        gradient = cotangent[member]
        second_sum = second_sum + filter_term(gradient, second_spread)
        second_mixed = unmix(second_weight, gradient)
        activation_grad = back_second(second_mixed.astype(jnp.float32))[0].astype(jnp.bfloat16)
        hidden_grad = jax.vjp(jax.nn.gelu, hidden)[1](activation_grad.astype(jnp.float32))[0].astype(jnp.bfloat16)
        first_sum = first_sum + filter_term(hidden_grad, first_spread)
        first_mixed = unmix(first_weight, hidden_grad)
        back_first = jax.vjp(partial(spread, stencil=stencil), source)[1]
        state_grads.append(back_first(first_mixed.astype(jnp.float32))[0].astype(jnp.bfloat16))
    grad_scale = 1.0 / math.sqrt(MEMBERS * NLAT * NLON)
    return (jnp.stack(outputs), jnp.stack(state_grads), first_sum * grad_scale, second_sum * grad_scale)
```

```python
import math

import jax
import jax.numpy as jnp
from jax import lax
from jax.experimental import pallas as pl
from jax.experimental.pallas import tpu as pltpu
from jax.sharding import PartitionSpec as P

MESH = pl.DeviceIdType.MESH
BF = jnp.bfloat16
F32 = jnp.float32

PIECE = 96


def dot(a, b, ca, cb):
    return lax.dot_general(a, b, (((ca,), (cb,)), ((), ())), preferred_element_type=F32)


def copy_to(src, dst, send, recv, device):
    return pltpu.make_async_remote_copy(
        src_ref=src, dst_ref=dst, send_sem=send, recv_sem=recv, device_id=device, device_id_type=MESH
    )


def tap_rows(quad, lat_off, lon_off, a, sign):
    lane = lax.broadcasted_iota(jnp.int32, (3, 128), 1)
    offset = jnp.where(lane < 64, lane, lane - 128) * sign
    total = jnp.zeros((3, 128), F32)
    for s in range(12):
        hit = (lon_off[:, s : s + 1] == offset) & (lat_off[:, s : s + 1] == a - 1)
        total = total + jnp.where(hit, quad[:, s : s + 1], 0.0)
    return total.astype(BF).astype(F32)


def banded(row, count, first, shift):
    wide = jnp.broadcast_to(row, (count, 128))
    return pltpu.roll(wide, (shift + first) % 128, 1, stride=1, stride_axis=0)


def main_band(row):
    block = banded(row, 128, 0, 0)
    gap = lax.broadcasted_iota(jnp.int32, (128, 128), 1) - lax.broadcasted_iota(jnp.int32, (128, 128), 0)
    return jnp.where((gap <= 4) & (gap >= -4), block, 0.0).astype(BF)


def edge_band(rows_of, first):
    total = jnp.zeros((16, 128), F32)
    lane = lax.broadcasted_iota(jnp.int32, (16, 128), 1)
    cell = lax.broadcasted_iota(jnp.int32, (16, 128), 0) + first
    for place, row in rows_of:
        t = lane - 32 * place
        block = banded(row, 16, first, 32 * place + 16)
        gap = jnp.where(t < 16, t - 16, t + 112) - cell
        ok = (t >= 0) & (t < 32) & (gap <= 4) & (gap >= -4)
        total = total + jnp.where(ok, block, 0.0)
    return total.astype(BF)


def kernel(
    x_ref, g_ref, w1_ref, w2_ref, quad_ref, lato_ref, lono_ref,
    lo_ref, sg_ref, d1_ref, d2_ref,
    ext1, ext2, bsend, brecv, bandf, banda, u_ref, t_ref, slope,
    gs, crecv, xs, xrecv, zrecv, zgroup, fin,
    s1, r1, s2, r2, sc, rc, sx, rx, sz, rz, sf, rf, sa, ra, sd, rd,
):
    e, l, x = lax.axis_index("ens"), lax.axis_index("lat"), lax.axis_index("lon")
    yh, core = e // 2, e % 2
    z, yl = l // 2, l % 2
    y = yh * 2 + yl
    me = y * 4 + x
    p, grp = z % 4, z // 4
    up, down = (l + 31) % 32, (l + 1) % 32
    left, right = (x + 3) % 4, (x + 1) % 4
    partner = (yh * 2 + 1 - core, l, x)

    def xy_peer(s):
        xx, yy = (x + s % 4) % 4, (y + s // 4) % 4
        return yy * 4 + xx, ((yy // 2) * 2 + core, z * 2 + yy % 2, xx)

    def z_device(zz):
        return (e, zz * 2 + yl, x)

    barrier = pltpu.get_barrier_semaphore()

    def hello(device):
        pl.semaphore_signal(barrier, inc=1, device_id=device, device_id_type=MESH)

    for ll, xx in ((up, x), (down, x), (l, left), (l, right), (up, left), (up, right), (down, left), (down, right)):
        hello((e, ll, xx))
    hello(partner)

    def hello_xy(s, c):
        hello(xy_peer(s)[1])
        return c

    lax.fori_loop(1, 16, hello_xy, 0)

    def hello_z(s, c):
        hello(z_device((z + s) % 16))
        return c

    lax.fori_loop(1, 16, hello_z, 0)

    ext1[0, 1:3] = x_ref[...].reshape(2, 4, 32, 256)
    ext1[1, 1:3] = g_ref[...].reshape(2, 4, 32, 256)
    taps = [(quad_ref[i], lato_ref[i], lono_ref[i]) for i in range(2)]
    adj = [[tap_rows(*taps[i], a, -1) for a in range(3)] for i in range(2)]
    bsend[...] = jnp.zeros((2, 8, 128), F32)
    bsend[0, 0:3] = adj[0][0]
    bsend[1, 0:3] = adj[1][2]

    pl.semaphore_wait(barrier, 8 + 1 + 15 + 15)

    first = [
        copy_to(bsend.at[0], brecv.at[1], s1.at[0], r1.at[0], (e, up, x)),
        copy_to(bsend.at[1], brecv.at[0], s1.at[1], r1.at[1], (e, down, x)),
        copy_to(ext1.at[0, 1], ext1.at[0, 4], s1.at[2], r1.at[2], (e, up, x)),
        copy_to(ext1.at[0, 2], ext1.at[0, 0], s1.at[3], r1.at[3], (e, down, x)),
    ]

    def edges(ext, s, r, n):
        return [
            copy_to(ext.at[:, 1:3, 3, 16:32], ext.at[:, 3, 1:3, 0:16], s.at[n], r.at[n], (e, l, right)),
            copy_to(ext.at[:, 1:3, 0, 0:16], ext.at[:, 3, 1:3, 16:32], s.at[n + 1], r.at[n + 1], (e, l, left)),
            copy_to(ext.at[:, 2, 3, 16:32], ext.at[:, 3, 0, 0:16], s.at[n + 2], r.at[n + 2], (e, down, right)),
            copy_to(ext.at[:, 2, 0, 0:16], ext.at[:, 3, 0, 16:32], s.at[n + 3], r.at[n + 3], (e, down, left)),
            copy_to(ext.at[:, 1, 3, 16:32], ext.at[:, 3, 3, 0:16], s.at[n + 4], r.at[n + 4], (e, up, right)),
            copy_to(ext.at[:, 1, 0, 0:16], ext.at[:, 3, 3, 16:32], s.at[n + 5], r.at[n + 5], (e, up, left)),
        ]

    first += edges(ext1, s1, r1, 6)
    first += [
        copy_to(ext1.at[1, 1], ext1.at[1, 4], s1.at[4], r1.at[4], (e, up, x)),
        copy_to(ext1.at[1, 2], ext1.at[1, 0], s1.at[5], r1.at[5], (e, down, x)),
    ]
    for c in first:
        c.start()

    top, bottom = (l > 0).astype(F32), (l < 31).astype(F32)
    col = ((0, 1, 2, 3), (0, 1, 3, 2))

    def put_bands(band, i, rows):
        for k in range(3):
            out = slice(k * 128, k * 128 + 128)
            for n in range(3):
                c = col[i][n] * 128
                band[i, out, c : c + 128] = main_band(rows[n][k : k + 1])
            c = col[i][3] * 128
            places = [(i + n, rows[n][k : k + 1]) for n in range(3)]
            band[i, k * 128 : k * 128 + 16, c : c + 128] = edge_band(places, 0)
            band[i, k * 128 + 16 : k * 128 + 112, c : c + 128] = jnp.zeros((96, 128), BF)
            band[i, k * 128 + 112 : k * 128 + 128, c : c + 128] = edge_band(places, 112)

    fwd = [[tap_rows(*taps[i], a, 1) for a in range(3)] for i in range(2)]
    put_bands(bandf, 0, [fwd[0][0] * top, fwd[0][1], fwd[0][2]])
    put_bands(bandf, 1, [fwd[1][0], fwd[1][1], fwd[1][2] * bottom])
    first[0].wait_recv()
    first[1].wait_recv()
    put_bands(banda, 0, [brecv[0, 0:3] * top, adj[0][1], adj[1][0]])
    put_bands(banda, 1, [adj[0][2], adj[1][1], brecv[1, 0:3] * bottom])

    def spread(band, ext, f, out):
        for i in range(2):
            cells = ext[f, i : i + 4].reshape(512, 256)
            got = dot(band[i], cells, 1, 0).astype(BF)
            for k in range(3):
                out[k, i * 128 : i * 128 + 128] = got[k * 128 : k * 128 + 128]

    def mixed(spreaded, weight, cw):
        total = dot(spreaded[0], weight[0], 1, cw)
        for k in range(1, 3):
            total = total + dot(spreaded[k], weight[k], 1, cw)
        return total

    for c in first[2:10]:
        c.wait_recv()
    spread(bandf, ext1, 0, u_ref)
    hidden = mixed(u_ref, w1_ref, 1)
    root = math.sqrt(2.0 / math.pi)
    square = hidden * hidden
    bend = jnp.tanh(root * hidden * (1.0 + 0.044715 * square))
    act = (0.5 * hidden * (1.0 + bend)).astype(BF)
    slope[...] = 0.5 * (1.0 + bend) + (0.5 * root) * hidden * (1.0 - bend * bend) * (1.0 + (3 * 0.044715) * square)
    ext2[0, 1:3] = act.reshape(2, 4, 32, 256)
    second = [
        copy_to(ext2.at[0, 1], ext2.at[0, 4], s2.at[0], r2.at[0], (e, up, x)),
        copy_to(ext2.at[0, 2], ext2.at[0, 0], s2.at[1], r2.at[1], (e, down, x)),
        copy_to(ext2.at[1, 1], ext2.at[1, 4], s2.at[2], r2.at[2], (e, up, x)),
        copy_to(ext2.at[1, 2], ext2.at[1, 0], s2.at[3], r2.at[3], (e, down, x)),
    ]
    second += edges(ext2, s2, r2, 4)
    second[0].start()
    second[1].start()

    first[10].wait_recv()
    first[11].wait_recv()
    spread(banda, ext1, 1, t_ref)

    def put_grad(row, value):
        value = value.astype(BF)
        gs[0, row : row + 256] = value[:, :128]
        gs[1, row : row + 256] = value[:, 128:]

    for k in range(3):
        put_grad(768 + k * 256, dot(t_ref[k], act, 0, 0))
    core2 = copy_to(gs.at[1 - core, 768:1536], crecv.at[768:1536], sc.at[0], rc.at[0], partner)
    core2.start()
    act_grad = mixed(t_ref, w2_ref, 0).astype(BF).astype(F32)
    hid_grad = (act_grad * slope[...]).astype(BF)
    ext2[1, 1:3] = hid_grad.reshape(2, 4, 32, 256)
    for k in range(3):
        put_grad(k * 256, dot(hid_grad, u_ref[k], 0, 0))
    core1 = copy_to(gs.at[1 - core, 0:768], crecv.at[0:768], sc.at[1], rc.at[1], partner)
    core1.start()

    core2.wait_recv()
    xs[768:1536] = (gs[core, 768:1536].astype(F32) + crecv[768:1536].astype(F32)).astype(BF)
    core1.wait_recv()
    xs[0:768] = (gs[core, 0:768].astype(F32) + crecv[0:768].astype(F32)).astype(BF)

    def piece(s):
        peer, device = xy_peer(s)
        rows = pl.ds(pl.multiple_of(peer * PIECE, 16), PIECE)
        return copy_to(xs.at[rows], xrecv.at[s - 1], sx.at[s - 1], rx.at[s - 1], device)

    def send_piece(s, c):
        piece(s).start()
        return c

    lax.fori_loop(1, 16, send_piece, 0)
    for c in second[2:]:
        c.start()

    mine = pl.ds(pl.multiple_of(me * PIECE, 16), PIECE)

    def add_piece(s, total):
        piece(s).wait_recv()
        return total + xrecv[s - 1].astype(F32)

    total = lax.fori_loop(1, 16, add_piece, xs[mine].astype(F32))
    zrecv[p] = total.astype(BF)

    def near(s):
        return copy_to(zrecv.at[p], zrecv.at[p], sz.at[s - 1], rz.at[p], z_device(grp * 4 + (p + s) % 4))

    def near_in(s):
        q = (p + s) % 4
        return copy_to(zrecv.at[q], zrecv.at[q], sz.at[s - 1], rz.at[q], z_device(grp * 4 + q))

    for s in range(1, 4):
        near(s).start()

    for n in (0, 1, 4, 5, 6, 7, 8, 9):
        second[n].wait_recv()
    core2.wait_send()
    core1.wait_send()
    for c in first:
        c.wait_send()
    for s in range(1, 4):
        near_in(s).wait_recv()
    total = zrecv[0].astype(F32)
    for q in range(1, 4):
        total = total + zrecv[q].astype(F32)
    zgroup[grp] = total.astype(BF)

    def far(n, group, member):
        return copy_to(zgroup.at[grp], zgroup.at[grp], sf.at[n], rf.at[grp], z_device(group * 4 + member))

    to_left = [((grp + 3) % 4, 3), ((grp + 3) % 4, 2), ((grp + 3) % 4, 1), ((grp + 3) % 4, 0), ((grp + 2) % 4, 3), ((grp + 2) % 4, 2)]
    to_right = [((grp + 1) % 4, 0), ((grp + 1) % 4, 1), ((grp + 1) % 4, 2), ((grp + 1) % 4, 3), ((grp + 2) % 4, 0), ((grp + 2) % 4, 1)]

    @pl.when(p == 0)
    def _():
        for n in (4, 5, 3, 2, 1, 0):
            far(n, *to_left[n]).start()

    @pl.when(p == 3)
    def _():
        for n in (4, 5, 3, 2, 1, 0):
            far(n, *to_right[n]).start()

    spread(bandf, ext2, 0, u_ref)
    lo_ref[...] = mixed(u_ref, w2_ref, 1).astype(BF)
    second[2].wait_recv()
    second[3].wait_recv()
    spread(banda, ext2, 1, t_ref)
    sg_ref[...] = mixed(t_ref, w1_ref, 0).astype(BF)

    for s in range(1, 4):
        q = (grp + s) % 4
        copy_to(zgroup.at[q], zgroup.at[q], sf.at[0], rf.at[q], z_device(q * 4)).wait_recv()
    total = zgroup[0].astype(F32)
    for q in range(1, 4):
        total = total + zgroup[q].astype(F32)
    fin[core, mine] = total.astype(BF)

    def spread_piece(s):
        return copy_to(fin.at[core, mine], fin.at[core, mine], sa.at[s - 1], ra.at[s - 1], xy_peer(s)[1])

    def send_back(s, c):
        spread_piece(s).start()
        return c

    lax.fori_loop(1, 16, send_back, 0)

    def wait_back(s, c):
        spread_piece(s).wait_recv()
        return c

    lax.fori_loop(1, 16, wait_back, 0)
    swap = copy_to(fin.at[core], fin.at[core], sd.at[0], rd.at[0], partner)
    swap.start()

    for c in second:
        c.wait_send()

    def wait_sent(s, c):
        piece(s).wait_send()
        spread_piece(s).wait_send()
        return c

    lax.fori_loop(1, 16, wait_sent, 0)
    for s in range(1, 4):
        near(s).wait_send()

    @pl.when(p == 0)
    def _():
        for n in range(6):
            far(n, *to_left[n]).wait_send()

    @pl.when(p == 3)
    def _():
        for n in range(6):
            far(n, *to_right[n]).wait_send()

    swap.wait_recv()
    scale = 1.0 / math.sqrt(4 * 64 * 512)
    for h in range(2):
        d1_ref[:, h * 128 : h * 128 + 128] = fin[h, 0:768].astype(F32) * scale
        d2_ref[:, h * 128 : h * 128 + 128] = fin[h, 768:1536].astype(F32) * scale
    swap.wait_send()


def body(state_field, first_weight, second_weight, quadrature, lat_offsets, lon_offsets, cotangent):
    def turned(field):
        return jnp.transpose(field[0], (1, 2, 0)).reshape(256, 256)

    def back(field):
        return jnp.transpose(field.reshape(2, 128, 256), (2, 0, 1))[None]

    vmem = pl.BlockSpec(memory_space=pltpu.VMEM)
    dma = pltpu.SemaphoreType.DMA
    lo, sg, d1, d2 = pl.pallas_call(
        kernel,
        out_shape=(
            jax.ShapeDtypeStruct((256, 256), BF),
            jax.ShapeDtypeStruct((256, 256), BF),
            jax.ShapeDtypeStruct((768, 256), F32),
            jax.ShapeDtypeStruct((768, 256), F32),
        ),
        in_specs=[vmem] * 7,
        out_specs=[vmem] * 4,
        scratch_shapes=[
            pltpu.VMEM((2, 5, 4, 32, 256), BF),
            pltpu.VMEM((2, 5, 4, 32, 256), BF),
            pltpu.VMEM((2, 8, 128), F32),
            pltpu.VMEM((2, 8, 128), F32),
            pltpu.VMEM((2, 384, 512), BF),
            pltpu.VMEM((2, 384, 512), BF),
            pltpu.VMEM((3, 256, 256), BF),
            pltpu.VMEM((3, 256, 256), BF),
            pltpu.VMEM((256, 256), F32),
            pltpu.VMEM((2, 1536, 128), BF),
            pltpu.VMEM((1536, 128), BF),
            pltpu.VMEM((1536, 128), BF),
            pltpu.VMEM((15, PIECE, 128), BF),
            pltpu.VMEM((4, PIECE, 128), BF),
            pltpu.VMEM((4, PIECE, 128), BF),
            pltpu.VMEM((2, 1536, 128), BF),
            dma((12,)), dma((12,)),
            dma((10,)), dma((10,)),
            dma((2,)), dma((2,)),
            dma((15,)), dma((15,)),
            dma((3,)), dma((4,)),
            dma((6,)), dma((4,)),
            dma((15,)), dma((15,)),
            dma((1,)), dma((1,)),
        ],
        compiler_params=pltpu.CompilerParams(collective_id=0, has_side_effects=True, vmem_limit_bytes=48 * 2**20),
        cost_estimate=pl.CostEstimate(flops=1_500_000_000, bytes_accessed=4_000_000, transcendentals=65536),
        name="conv_pair",
    )(turned(state_field), turned(cotangent), first_weight, second_weight, quadrature, lat_offsets, lon_offsets)
    return back(lo), back(sg), d1.reshape(3, 256, 256), d2.reshape(3, 256, 256)


def solution(mesh):
    in_specs = (
        P("ens", None, "lat", "lon"),
        P(),
        P(),
        P("lat", None, None),
        P("lat", None, None),
        P("lat", None, None),
        P("ens", None, "lat", "lon"),
    )
    out_specs = (P("ens", None, "lat", "lon"), P("ens", None, "lat", "lon"), P(), P())
    return jax.shard_map(body, mesh=mesh, in_specs=in_specs, out_specs=out_specs, check_vma=False)
```

```python
import math

import jax
import jax.numpy as jnp
from jax import lax
from jax.experimental import pallas as pl
from jax.experimental.pallas import tpu as pltpu
from jax.sharding import PartitionSpec as P

MESH = pl.DeviceIdType.MESH
BF = jnp.bfloat16
F32 = jnp.float32

PIECE = 48


def dot(a, b, ca, cb):
    return lax.dot_general(a, b, (((ca,), (cb,)), ((), ())), preferred_element_type=F32)


def copy_to(src, dst, send, recv, device):
    return pltpu.make_async_remote_copy(
        src_ref=src, dst_ref=dst, send_sem=send, recv_sem=recv, device_id=device, device_id_type=MESH
    )


def tap_rows(quad, lat_off, lon_off, a, sign):
    lane = lax.broadcasted_iota(jnp.int32, (3, 128), 1)
    offset = jnp.where(lane < 64, lane, lane - 128) * sign
    total = jnp.zeros((3, 128), F32)
    for s in range(12):
        hit = (lon_off[:, s : s + 1] == offset) & (lat_off[:, s : s + 1] == a - 1)
        total = total + jnp.where(hit, quad[:, s : s + 1], 0.0)
    return total.astype(BF).astype(F32)


def banded(row, count, first, shift):
    wide = jnp.broadcast_to(row, (count, 128))
    return pltpu.roll(wide, (shift + first) % 128, 1, stride=1, stride_axis=0)


def main_band(row):
    block = banded(row, 128, 0, 0)
    gap = lax.broadcasted_iota(jnp.int32, (128, 128), 1) - lax.broadcasted_iota(jnp.int32, (128, 128), 0)
    return jnp.where((gap <= 4) & (gap >= -4), block, 0.0).astype(BF)


def edge_band(rows_of, first):
    total = jnp.zeros((16, 128), F32)
    lane = lax.broadcasted_iota(jnp.int32, (16, 128), 1)
    cell = lax.broadcasted_iota(jnp.int32, (16, 128), 0) + first
    for place, row in rows_of:
        t = lane - 32 * place
        block = banded(row, 16, first, 32 * place + 16)
        gap = jnp.where(t < 16, t - 16, t + 112) - cell
        ok = (t >= 0) & (t < 32) & (gap <= 4) & (gap >= -4)
        total = total + jnp.where(ok, block, 0.0)
    return total.astype(BF)


def kernel(
    x_hbm, g_hbm, w1_hbm, w2_hbm, quad_hbm, lato_hbm, lono_hbm,
    lo_hbm, sg_hbm, fin_hbm,
    lo_ref, sg_ref, fin, xg, w1_ref, w2_ref, quad_ref, lato_ref, lono_ref, sel,
    ext1, ext2, bsend, brecv, bandf, banda, u_ref, t_ref, slope,
    gs, crecv, xs, xrecv, zrecv, zgroup,
    si, s1, r1, s2, r2, sc, rc, sx, rx, sz, rz, sf, rf, sa, ra, sd, rd, so, tok,
):
    e, l, x = lax.axis_index("ens"), lax.axis_index("lat"), lax.axis_index("lon")
    yh, core = e // 2, e % 2
    z, yl = l // 2, l % 2
    y = yh * 2 + yl
    me = y * 4 + x
    p, grp = z % 4, z // 4
    up, down = (l + 31) % 32, (l + 1) % 32
    left, right = (x + 3) % 4, (x + 1) % 4
    partner = (yh * 2 + 1 - core, l, x)
    across = ((1 - yh) * 2 + core, z * 2 + 1 - yl, x)

    def xy_peer(s):
        xx, yy = (x + s % 4) % 4, (y + s // 4) % 4
        return yy * 4 + xx, ((yy // 2) * 2 + core, z * 2 + yy % 2, xx)

    def z_device(zz):
        return (e, zz * 2 + yl, x)

    barrier = pltpu.get_barrier_semaphore()

    def signal(sem, device):
        pl.semaphore_signal(sem, inc=1, device_id=device, device_id_type=MESH)

    for ll, xx in ((up, x), (down, x), (l, left), (l, right), (up, left), (up, right), (down, left), (down, right)):
        signal(barrier, (e, ll, xx))
    signal(barrier, partner)
    signal(barrier, across)

    loads = [
        pltpu.make_async_copy(src, dst, si.at[n])
        for n, (src, dst) in enumerate(
            (
                (x_hbm, xg.at[0]), (quad_hbm, quad_ref), (lato_hbm, lato_ref), (lono_hbm, lono_ref),
                (g_hbm, xg.at[1]), (w1_hbm, w1_ref), (w2_hbm, w2_ref),
            )
        )
    ]
    for c in loads:
        c.start()

    for r in range(2):
        at = lax.broadcasted_iota(jnp.int32, (512, 256), 0)
        want = 2 * lax.broadcasted_iota(jnp.int32, (512, 256), 1) + r
        sel[r] = jnp.where(at == want, 1.0, 0.0).astype(BF)

    def turn(f):
        for r in range(2):
            ext1[f, 1 + r] = dot(xg[f], sel[r], 0, 0).astype(BF).reshape(4, 32, 256)

    loads[0].wait()
    turn(0)
    for n in (1, 2, 3):
        loads[n].wait()
    taps = [(quad_ref[:, i], lato_ref[:, i], lono_ref[:, i]) for i in range(2)]
    adj = [[tap_rows(*taps[i], a, -1) for a in range(3)] for i in range(2)]
    bsend[...] = jnp.zeros((2, 8, 128), F32)
    bsend[0, 0:3] = adj[0][0]
    bsend[1, 0:3] = adj[1][2]
    loads[4].wait()
    turn(1)

    pl.semaphore_wait(barrier, 10)

    first = [
        copy_to(bsend.at[0], brecv.at[1], s1.at[0], r1.at[0], (e, up, x)),
        copy_to(bsend.at[1], brecv.at[0], s1.at[1], r1.at[1], (e, down, x)),
        copy_to(ext1.at[0, 1], ext1.at[0, 4], s1.at[2], r1.at[2], (e, up, x)),
        copy_to(ext1.at[0, 2], ext1.at[0, 0], s1.at[3], r1.at[3], (e, down, x)),
    ]

    def edges(ext, s, r, n):
        return [
            copy_to(ext.at[:, 1:3, 3, 16:32], ext.at[:, 3, 1:3, 0:16], s.at[n], r.at[n], (e, l, right)),
            copy_to(ext.at[:, 1:3, 0, 0:16], ext.at[:, 3, 1:3, 16:32], s.at[n + 1], r.at[n + 1], (e, l, left)),
            copy_to(ext.at[:, 2, 3, 16:32], ext.at[:, 3, 0, 0:16], s.at[n + 2], r.at[n + 2], (e, down, right)),
            copy_to(ext.at[:, 2, 0, 0:16], ext.at[:, 3, 0, 16:32], s.at[n + 3], r.at[n + 3], (e, down, left)),
            copy_to(ext.at[:, 1, 3, 16:32], ext.at[:, 3, 3, 0:16], s.at[n + 4], r.at[n + 4], (e, up, right)),
            copy_to(ext.at[:, 1, 0, 0:16], ext.at[:, 3, 3, 16:32], s.at[n + 5], r.at[n + 5], (e, up, left)),
        ]

    first += edges(ext1, s1, r1, 6)
    first += [
        copy_to(ext1.at[1, 1], ext1.at[1, 4], s1.at[4], r1.at[4], (e, up, x)),
        copy_to(ext1.at[1, 2], ext1.at[1, 0], s1.at[5], r1.at[5], (e, down, x)),
    ]
    for c in first:
        c.start()
    for device in ((e, up, x), (e, down, x), (e, l, left), (e, l, right), across):
        signal(tok.at[0], device)

    top, bottom = (l > 0).astype(F32), (l < 31).astype(F32)
    col = ((0, 1, 2, 3), (0, 1, 3, 2))

    def put_bands(band, i, rows):
        for k in range(3):
            out = slice(k * 128, k * 128 + 128)
            for n in range(3):
                c = col[i][n] * 128
                band[i, out, c : c + 128] = main_band(rows[n][k : k + 1])
            c = col[i][3] * 128
            places = [(i + n, rows[n][k : k + 1]) for n in range(3)]
            band[i, k * 128 : k * 128 + 16, c : c + 128] = edge_band(places, 0)
            band[i, k * 128 + 16 : k * 128 + 112, c : c + 128] = jnp.zeros((96, 128), BF)
            band[i, k * 128 + 112 : k * 128 + 128, c : c + 128] = edge_band(places, 112)

    fwd = [[tap_rows(*taps[i], a, 1) for a in range(3)] for i in range(2)]
    put_bands(bandf, 0, [fwd[0][0] * top, fwd[0][1], fwd[0][2]])
    put_bands(bandf, 1, [fwd[1][0], fwd[1][1], fwd[1][2] * bottom])
    pl.semaphore_wait(tok.at[0], 5)
    two = (e, l, (x + 2) % 4), ((1 - yh) * 2 + core, l, x), z_device((z + 1) % 16), z_device((z + 15) % 16)
    for device in two:
        signal(tok.at[1], device)
    first[0].wait_recv()
    first[1].wait_recv()
    put_bands(banda, 0, [brecv[0, 0:3] * top, adj[0][1], adj[1][0]])
    put_bands(banda, 1, [adj[0][2], adj[1][1], brecv[1, 0:3] * bottom])

    def spread(band, ext, f, out):
        for i in range(2):
            cells = ext[f, i : i + 4].reshape(512, 256)
            got = dot(band[i], cells, 1, 0).astype(BF)
            for k in range(3):
                out[k, i * 128 : i * 128 + 128] = got[k * 128 : k * 128 + 128]

    def mixed(spreaded, weight, cw):
        total = dot(spreaded[0], weight[0], 1, cw)
        for k in range(1, 3):
            total = total + dot(spreaded[k], weight[k], 1, cw)
        return total

    loads[5].wait()
    loads[6].wait()
    for c in first[2:10]:
        c.wait_recv()
    spread(bandf, ext1, 0, u_ref)
    hidden = mixed(u_ref, w1_ref, 1)
    root = math.sqrt(2.0 / math.pi)
    square = hidden * hidden
    bend = jnp.tanh(root * hidden * (1.0 + 0.044715 * square))
    act = (0.5 * hidden * (1.0 + bend)).astype(BF)
    slope[...] = 0.5 * (1.0 + bend) + (0.5 * root) * hidden * (1.0 - bend * bend) * (1.0 + (3 * 0.044715) * square)
    ext2[0, 1:3] = act.reshape(2, 4, 32, 256)

    first[10].wait_recv()
    first[11].wait_recv()
    spread(banda, ext1, 1, t_ref)

    def put_grad(ch, row, value):
        value = value.astype(BF)
        gs[ch, 0, row : row + 256] = value[:, :128]
        gs[ch, 1, row : row + 256] = value[:, 128:]

    cores = [
        copy_to(gs.at[ch, 1 - core], crecv.at[ch], sc.at[ch], rc.at[ch], partner) for ch in range(2)
    ]
    for k in range(3):
        put_grad(0, k * 256, dot(t_ref[k], act, 0, 0))
    cores[0].start()
    act_grad = mixed(t_ref, w2_ref, 0).astype(BF).astype(F32)
    hid_grad = (act_grad * slope[...]).astype(BF)
    ext2[1, 1:3] = hid_grad.reshape(2, 4, 32, 256)
    for k in range(3):
        put_grad(1, k * 256, dot(hid_grad, u_ref[k], 0, 0))
    cores[1].start()
    pl.semaphore_wait(tok.at[1], 4)
    for d in (2, 14):
        signal(tok.at[2], z_device((z + d) % 16))

    def piece(ch, s):
        peer, device = xy_peer(s)
        rows = pl.ds(pl.multiple_of(peer * PIECE, 16), PIECE)
        return copy_to(xs.at[ch, rows], xrecv.at[ch, s - 1], sx.at[ch, s - 1], rx.at[ch, s - 1], device)

    for ch in range(2):
        cores[ch].wait_recv()
        xs[ch] = (gs[ch, core].astype(F32) + crecv[ch].astype(F32)).astype(BF)

        def send_piece(s, c, ch=ch):
            piece(ch, s).start()
            return c

        lax.fori_loop(1, 16, send_piece, 0)

    pl.semaphore_wait(tok.at[2], 2)
    for d in (4, 12):
        signal(tok.at[3], z_device((z + d) % 16))

    mine = pl.ds(pl.multiple_of(me * PIECE, 16), PIECE)

    def near(ch, s):
        return copy_to(zrecv.at[ch, p], zrecv.at[ch, p], sz.at[ch, s - 1], rz.at[ch, p], z_device(grp * 4 + (p + s) % 4))

    def near_in(ch, s):
        q = (p + s) % 4
        return copy_to(zrecv.at[ch, q], zrecv.at[ch, q], sz.at[ch, s - 1], rz.at[ch, q], z_device(grp * 4 + q))

    for ch in range(2):

        def add_piece(s, total, ch=ch):
            piece(ch, s).wait_recv()
            return total + xrecv[ch, s - 1].astype(F32)

        zrecv[ch, p] = lax.fori_loop(1, 16, add_piece, xs[ch, mine].astype(F32)).astype(BF)
        for s in range(1, 4):
            near(ch, s).start()

    second = [
        copy_to(ext2.at[:, 1], ext2.at[:, 4], s2.at[0], r2.at[0], (e, up, x)),
        copy_to(ext2.at[:, 2], ext2.at[:, 0], s2.at[1], r2.at[1], (e, down, x)),
    ]
    second += edges(ext2, s2, r2, 2)
    for c in second:
        c.start()

    def far(ch, n, group, member):
        return copy_to(
            zgroup.at[ch, grp], zgroup.at[ch, grp], sf.at[ch, n], rf.at[ch, grp], z_device(group * 4 + member)
        )

    before, after, opposite = (grp + 3) % 4, (grp + 1) % 4, (grp + 2) % 4
    to_left = [(opposite, 2), (opposite, 3), (before, 0), (before, 1), (before, 2), (before, 3)]
    to_right = [(opposite, 1), (opposite, 0), (after, 3), (after, 2), (after, 1), (after, 0)]

    def all_four(ref):
        total = ref[0].astype(F32)
        for q in range(1, 4):
            total = total + ref[q].astype(F32)
        return total.astype(BF)

    pl.semaphore_wait(tok.at[3], 2)
    for ch in range(2):
        for s in range(1, 4):
            near_in(ch, s).wait_recv()
        zgroup[ch, grp] = all_four(zrecv.at[ch])

        @pl.when(p == 0)
        def _(ch=ch):
            for n in range(6):
                far(ch, n, *to_left[n]).start()

        @pl.when(p == 3)
        def _(ch=ch):
            for n in range(6):
                far(ch, n, *to_right[n]).start()

    def spread_piece(ch, s):
        cells = fin.at[ch, core, mine]
        return copy_to(cells, cells, sa.at[ch, s - 1], ra.at[ch, s - 1], xy_peer(s)[1])

    for ch in range(2):
        for s in range(1, 4):
            q = (grp + s) % 4
            cells = zgroup.at[ch, q]
            copy_to(cells, cells, sf.at[ch, 0], rf.at[ch, q], z_device(q * 4)).wait_recv()
        fin[ch, core, mine] = all_four(zgroup.at[ch])

        def send_back(s, c, ch=ch):
            spread_piece(ch, s).start()
            return c

        lax.fori_loop(1, 16, send_back, 0)

    def turned_back(cells):
        return (dot(sel[0], cells[0:128], 1, 1) + dot(sel[1], cells[128:256], 1, 1)).astype(BF)

    for c in second:
        c.wait_recv()
    spread(bandf, ext2, 0, u_ref)
    lo_ref[...] = turned_back(mixed(u_ref, w2_ref, 1).astype(BF))
    spread(banda, ext2, 1, t_ref)
    sg_ref[...] = turned_back(mixed(t_ref, w1_ref, 0).astype(BF))
    stores = [
        pltpu.make_async_copy(lo_ref, lo_hbm, so.at[0]),
        pltpu.make_async_copy(sg_ref, sg_hbm, so.at[1]),
        pltpu.make_async_copy(fin.at[0], fin_hbm.at[0], so.at[2]),
        pltpu.make_async_copy(fin.at[1], fin_hbm.at[1], so.at[3]),
    ]
    stores[0].start()
    stores[1].start()

    for c in first + second + cores:
        c.wait_send()
    for ch in range(2):

        def wait_sent(s, c, ch=ch):
            piece(ch, s).wait_send()
            return c

        lax.fori_loop(1, 16, wait_sent, 0)
        for s in range(1, 4):
            near(ch, s).wait_send()

        @pl.when(p == 0)
        def _(ch=ch):
            for n in range(6):
                far(ch, n, *to_left[n]).wait_send()

        @pl.when(p == 3)
        def _(ch=ch):
            for n in range(6):
                far(ch, n, *to_right[n]).wait_send()

    swaps = [copy_to(fin.at[ch, core], fin.at[ch, core], sd.at[ch], rd.at[ch], partner) for ch in range(2)]
    for ch in range(2):

        def wait_back(s, c, ch=ch):
            spread_piece(ch, s).wait()
            return c

        lax.fori_loop(1, 16, wait_back, 0)
        swaps[ch].start()
    for ch in range(2):
        swaps[ch].wait()
        stores[2 + ch].start()
    for c in stores:
        c.wait()


def finish(lo_in, sg_in, fin_in, lo_hbm, sg_hbm, d1_hbm, d2_hbm, cells, fin, d_ref, sems):
    pieces = [(n, k) for n in range(2) for k in range(3)]
    loads, stores = [], []
    for n, k in pieces:
        rows = slice(k * 256, k * 256 + 256)
        loads.append(pltpu.make_async_copy(fin_in.at[n, :, rows], fin.at[n, k], sems.at[3 * n + k]))
        loads[-1].start()
    for n, (src, dst) in enumerate(((lo_in, lo_hbm), (sg_in, sg_hbm))):
        loads.append(pltpu.make_async_copy(src, cells.at[n], sems.at[6 + n]))
        loads[-1].start()
        stores.append(pltpu.make_async_copy(cells.at[n], dst, sems.at[14 + n]))
    scale = 1.0 / math.sqrt(4 * 64 * 512)
    for (n, k), load in zip(pieces, loads):
        load.wait()
        for h in range(2):
            d_ref[n, k, :, h * 128 : h * 128 + 128] = fin[n, k, h].astype(F32) * scale
        stores.append(pltpu.make_async_copy(d_ref.at[n, k], (d2_hbm, d1_hbm)[n].at[k], sems.at[8 + 3 * n + k]))
        stores[-1].start()
    for n in range(2):
        loads[6 + n].wait()
        stores[n].start()
    for c in stores:
        c.wait()


def body(state_field, first_weight, second_weight, quadrature, lat_offsets, lon_offsets, cotangent):
    anywhere = pl.BlockSpec(memory_space=pl.ANY)
    dma = pltpu.SemaphoreType.DMA
    lo, sg, fin = pl.pallas_call(
        kernel,
        out_shape=(
            jax.ShapeDtypeStruct((512, 128), BF),
            jax.ShapeDtypeStruct((512, 128), BF),
            jax.ShapeDtypeStruct((2, 2, 768, 128), BF),
        ),
        in_specs=[anywhere] * 7,
        out_specs=[anywhere] * 3,
        scratch_shapes=[
            pltpu.VMEM((512, 128), BF),
            pltpu.VMEM((512, 128), BF),
            pltpu.VMEM((2, 2, 768, 128), BF),
            pltpu.VMEM((2, 512, 128), BF),
            pltpu.VMEM((3, 256, 256), BF),
            pltpu.VMEM((3, 256, 256), BF),
            pltpu.VMEM((3, 2, 12), F32),
            pltpu.VMEM((3, 2, 12), jnp.int32),
            pltpu.VMEM((3, 2, 12), jnp.int32),
            pltpu.VMEM((2, 512, 256), BF),
            pltpu.VMEM((2, 5, 4, 32, 256), BF),
            pltpu.VMEM((2, 5, 4, 32, 256), BF),
            pltpu.VMEM((2, 8, 128), F32),
            pltpu.VMEM((2, 8, 128), F32),
            pltpu.VMEM((2, 384, 512), BF),
            pltpu.VMEM((2, 384, 512), BF),
            pltpu.VMEM((3, 256, 256), BF),
            pltpu.VMEM((3, 256, 256), BF),
            pltpu.VMEM((256, 256), F32),
            pltpu.VMEM((2, 2, 768, 128), BF),
            pltpu.VMEM((2, 768, 128), BF),
            pltpu.VMEM((2, 768, 128), BF),
            pltpu.VMEM((2, 15, PIECE, 128), BF),
            pltpu.VMEM((2, 4, PIECE, 128), BF),
            pltpu.VMEM((2, 4, PIECE, 128), BF),
            dma((7,)),
            dma((12,)), dma((12,)),
            dma((8,)), dma((8,)),
            dma((2,)), dma((2,)),
            dma((2, 15)), dma((2, 15)),
            dma((2, 3)), dma((2, 4)),
            dma((2, 6)), dma((2, 4)),
            dma((2, 15)), dma((2, 15)),
            dma((2,)), dma((2,)),
            dma((4,)),
            pltpu.SemaphoreType.REGULAR((4,)),
        ],
        compiler_params=pltpu.CompilerParams(collective_id=0, has_side_effects=True, vmem_limit_bytes=60 * 2**20),
        cost_estimate=pl.CostEstimate(flops=1_500_000_000, bytes_accessed=4_000_000, transcendentals=65536),
        name="conv_pair",
    )(
        state_field.reshape(512, 128),
        cotangent.reshape(512, 128),
        first_weight,
        second_weight,
        *(jnp.transpose(t, (1, 0, 2)) for t in (quadrature, lat_offsets, lon_offsets)),
    )
    lo, sg, d1, d2 = pl.pallas_call(
        finish,
        out_shape=(
            jax.ShapeDtypeStruct((512, 128), BF),
            jax.ShapeDtypeStruct((512, 128), BF),
            jax.ShapeDtypeStruct((3, 256, 256), F32),
            jax.ShapeDtypeStruct((3, 256, 256), F32),
        ),
        in_specs=[anywhere] * 3,
        out_specs=[anywhere] * 4,
        scratch_shapes=[
            pltpu.VMEM((2, 512, 128), BF),
            pltpu.VMEM((2, 3, 2, 256, 128), BF),
            pltpu.VMEM((2, 3, 256, 256), F32),
            dma((16,)),
        ],
        compiler_params=pltpu.CompilerParams(vmem_limit_bytes=60 * 2**20),
        name="put_out",
    )(lo, sg, fin)
    return lo.reshape(1, 256, 2, 128), sg.reshape(1, 256, 2, 128), d1, d2


def solution(mesh):
    in_specs = (
        P("ens", None, "lat", "lon"),
        P(),
        P(),
        P("lat", None, None),
        P("lat", None, None),
        P("lat", None, None),
        P("ens", None, "lat", "lon"),
    )
    out_specs = (P("ens", None, "lat", "lon"), P("ens", None, "lat", "lon"), P(), P())
    return jax.shard_map(body, mesh=mesh, in_specs=in_specs, out_specs=out_specs, check_vma=False)
```

```python
import math

import jax
import jax.numpy as jnp
from jax import lax
from jax.experimental import pallas as pl
from jax.experimental.pallas import tpu as pltpu
from jax.sharding import PartitionSpec as P

MESH = pl.DeviceIdType.MESH
BF = jnp.bfloat16
F32 = jnp.float32

PIECE = 48


def dot(a, b, ca, cb):
    return lax.dot_general(a, b, (((ca,), (cb,)), ((), ())), preferred_element_type=F32)


def copy_to(src, dst, send, recv, device):
    return pltpu.make_async_remote_copy(
        src_ref=src, dst_ref=dst, send_sem=send, recv_sem=recv, device_id=device, device_id_type=MESH
    )


def tap_rows(quad, lat_off, lon_off, sign):
    lane = lax.broadcasted_iota(jnp.int32, (8, 128), 1)
    code = 32 * (lat_off + 1) + sign * lon_off
    code = jnp.where(code < 0, code + 128, code)
    total = jnp.zeros((8, 128), F32)
    for s in range(12):
        total = total + jnp.where(lane == code[:, s : s + 1], quad[:, s : s + 1], 0.0)
    return total.astype(BF).astype(F32)


def one_tap(taps, a):
    lane = lax.broadcasted_iota(jnp.int32, (8, 128), 1)
    moved = taps if a == 0 else pltpu.roll(taps, 128 - 32 * a, 1)
    return jnp.where((lane < 5) | (lane > 123), moved, 0.0)


def banded(row, count, first, shift):
    wide = jnp.broadcast_to(row, (count, 128))
    return pltpu.roll(wide, (shift + first) % 128, 1, stride=1, stride_axis=0)


def put_main(band, i, out, c, row):
    block = banded(row, 128, 0, 0)
    lane = lax.broadcasted_iota(jnp.int32, (16, 128), 1)
    band[i, out : out + 16, c : c + 128] = jnp.where(lane < 64, block[0:16], 0.0).astype(BF)
    band[i, out + 16 : out + 112, c : c + 128] = block[16:112].astype(BF)
    band[i, out + 112 : out + 128, c : c + 128] = jnp.where(lane >= 64, block[112:128], 0.0).astype(BF)


def edge_band(rows_of, first):
    total = jnp.zeros((16, 128), F32)
    lane = lax.broadcasted_iota(jnp.int32, (16, 128), 1)
    for place, row in rows_of:
        t = lane - 32 * place
        block = banded(row, 16, first, 32 * place + 16)
        ok = (t >= 0) & (t < 16) if first == 0 else (t >= 16) & (t < 32)
        total = total + jnp.where(ok, block, 0.0)
    return total.astype(BF)


def kernel(
    x_hbm, g_hbm, w1_hbm, w2_hbm, quad_hbm, lato_hbm, lono_hbm,
    lo_ref, sg_ref, fin,
    xg, w1_ref, w2_ref, quad_ref, lato_ref, lono_ref, sel,
    ext1, ext2, bsend, brecv, bandf, banda, u_ref, t_ref, slope,
    gs, crecv, xs, xrecv, zrecv, zgroup,
    si, s1, r1, s2, r2, sc, rc, sx, rx, sz, rz, sf, rf, sa, ra, sd, rd, tok,
):
    e, l, x = lax.axis_index("ens"), lax.axis_index("lat"), lax.axis_index("lon")
    yh, core = e // 2, e % 2
    z, yl = l // 2, l % 2
    y = yh * 2 + yl
    me = y * 4 + x
    p, grp = z % 4, z // 4
    up, down = (l + 31) % 32, (l + 1) % 32
    left, right = (x + 3) % 4, (x + 1) % 4
    partner = (yh * 2 + 1 - core, l, x)
    across = ((1 - yh) * 2 + core, z * 2 + 1 - yl, x)

    def xy_peer(s):
        xx, yy = (x + s % 4) % 4, (y + s // 4) % 4
        return yy * 4 + xx, ((yy // 2) * 2 + core, z * 2 + yy % 2, xx)

    def far_first(n):
        def pick(i):
            return (2 + i + (i // 2) * (1 + 2 * (i % 2))) % 4

        return 4 * pick(n // 4) + pick(n % 4)

    def z_device(zz):
        return (e, zz * 2 + yl, x)

    loads = [
        pltpu.make_async_copy(src, dst, si.at[n])
        for n, (src, dst) in enumerate(
            (
                (x_hbm, xg.at[0]), (quad_hbm, quad_ref), (lato_hbm, lato_ref), (lono_hbm, lono_ref),
                (g_hbm, xg.at[1]), (w1_hbm, w1_ref), (w2_hbm, w2_ref),
            )
        )
    ]
    for c in loads:
        c.start()

    barrier = pltpu.get_barrier_semaphore()

    def signal(sem, device):
        pl.semaphore_signal(sem, inc=1, device_id=device, device_id_type=MESH)

    for ll, xx in ((up, x), (down, x), (l, left), (l, right), (up, left), (up, right), (down, left), (down, right)):
        signal(barrier, (e, ll, xx))
    signal(barrier, partner)
    signal(barrier, across)

    at = lax.broadcasted_iota(jnp.int32, (256, 256), 0)
    to = lax.broadcasted_iota(jnp.int32, (256, 256), 1)
    sel[...] = jnp.where(at == jnp.where(to < 128, 2 * to, 2 * to - 255), 1.0, 0.0).astype(BF)

    def turn(f):
        for h in range(2):
            got = dot(xg[f, h * 256 : h * 256 + 256], sel[...], 0, 0).astype(BF)
            for r in range(2):
                ext1[f, 1 + r, :, :, h * 128 : h * 128 + 128] = got[:, r * 128 : r * 128 + 128].reshape(4, 32, 128)

    def rows(ext, f, s, r, n):
        return [
            copy_to(ext.at[f, 1], ext.at[f, 4], s.at[n], r.at[n], (e, up, x)),
            copy_to(ext.at[f, 2], ext.at[f, 0], s.at[n + 1], r.at[n + 1], (e, down, x)),
        ]

    def edges(ext, f, s, r, n):
        return [
            copy_to(ext.at[f, 2, 3, 16:32], ext.at[f, 3, 0, 0:16], s.at[n], r.at[n], (e, down, right)),
            copy_to(ext.at[f, 2, 0, 0:16], ext.at[f, 3, 0, 16:32], s.at[n + 1], r.at[n + 1], (e, down, left)),
            copy_to(ext.at[f, 1, 3, 16:32], ext.at[f, 3, 3, 0:16], s.at[n + 2], r.at[n + 2], (e, up, right)),
            copy_to(ext.at[f, 1, 0, 0:16], ext.at[f, 3, 3, 16:32], s.at[n + 3], r.at[n + 3], (e, up, left)),
            copy_to(ext.at[f, 1:3, 3, 16:32], ext.at[f, 3, 1:3, 0:16], s.at[n + 4], r.at[n + 4], (e, l, right)),
            copy_to(ext.at[f, 1:3, 0, 0:16], ext.at[f, 3, 1:3, 16:32], s.at[n + 5], r.at[n + 5], (e, l, left)),
        ]

    first = [edges(ext1, f, s1, r1, 8 * f) + rows(ext1, f, s1, r1, 8 * f + 6) for f in range(2)]
    first.append(
        [
            copy_to(bsend, brecv.at[1], s1.at[16], r1.at[16], (e, up, x)),
            copy_to(bsend, brecv.at[0], s1.at[17], r1.at[17], (e, down, x)),
        ]
    )
    loads[0].wait()
    turn(0)
    pl.semaphore_wait(barrier, 10)
    for c in first[0]:
        c.start()
    loads[4].wait()
    turn(1)
    for c in first[1]:
        c.start()
    for n in (1, 2, 3):
        loads[n].wait()
    pad = jnp.zeros((2, 12), jnp.int32)
    lato = jnp.concatenate([lato_ref[:, 0], lato_ref[:, 1], pad])
    lono = jnp.concatenate([lono_ref[:, 0], lono_ref[:, 1], pad])
    quad = jnp.concatenate([quad_ref[:, 0], quad_ref[:, 1], pad.astype(F32)])
    adjoint = tap_rows(quad, lato, lono, -1)
    bsend[...] = adjoint
    for c in first[2]:
        c.start()
    for device in ((e, up, x), (e, down, x), (e, l, left), (e, l, right), across):
        signal(tok.at[0], device)

    top, bottom = (l > 0).astype(F32), (l < 31).astype(F32)
    col = ((0, 1, 2, 3), (0, 1, 3, 2))

    def put_bands(band, i, rows):
        for k in range(3):
            for n in range(3):
                put_main(band, i, k * 128, col[i][n] * 128, rows[n](k))
            c = col[i][3] * 128
            places = [(i + n, rows[n](k)) for n in range(3)]
            band[i, k * 128 : k * 128 + 16, c : c + 128] = edge_band(places, 0)
            band[i, k * 128 + 16 : k * 128 + 112, c : c + 128] = jnp.zeros((96, 128), BF)
            band[i, k * 128 + 112 : k * 128 + 128, c : c + 128] = edge_band(places, 112)

    def of(taps, i):
        return lambda k: taps[3 * i + k : 3 * i + k + 1]

    taps = tap_rows(quad, lato, lono, 1)
    fwd = [one_tap(taps, a) for a in range(3)]
    put_bands(bandf, 0, [of(fwd[0] * top, 0), of(fwd[1], 0), of(fwd[2], 0)])
    put_bands(bandf, 1, [of(fwd[0], 1), of(fwd[1], 1), of(fwd[2] * bottom, 1)])
    pl.semaphore_wait(tok.at[0], 5)
    two = (e, l, (x + 2) % 4), ((1 - yh) * 2 + core, l, x), z_device((z + 1) % 16), z_device((z + 15) % 16)
    for device in two:
        signal(tok.at[1], device)
    for c in first[2]:
        c.wait_recv()
    adj = [one_tap(adjoint, a) for a in range(3)]
    put_bands(banda, 0, [of(one_tap(brecv[0], 2) * top, 1), of(adj[1], 0), of(adj[0], 1)])
    put_bands(banda, 1, [of(adj[2], 0), of(adj[1], 1), of(one_tap(brecv[1], 0) * bottom, 0)])

    def spread(band, ext, f, out):
        for i in range(2):
            cells = ext[f, i : i + 4].reshape(512, 256)
            got = dot(band[i], cells, 1, 0).astype(BF)
            for k in range(3):
                out[k, i * 128 : i * 128 + 128] = got[k * 128 : k * 128 + 128]

    def mixed(spreaded, weight, cw):
        total = dot(spreaded[0], weight[0], 1, cw)
        for k in range(1, 3):
            total = total + dot(spreaded[k], weight[k], 1, cw)
        return total

    loads[5].wait()
    loads[6].wait()
    for c in first[0]:
        c.wait_recv()
    spread(bandf, ext1, 0, u_ref)
    hidden = mixed(u_ref, w1_ref, 1)
    root = math.sqrt(2.0 / math.pi)
    square = hidden * hidden
    bend = jnp.tanh(root * hidden * (1.0 + 0.044715 * square))
    act = (0.5 * hidden * (1.0 + bend)).astype(BF)
    slope[...] = 0.5 * (1.0 + bend) + (0.5 * root) * hidden * (1.0 - bend * bend) * (1.0 + (3 * 0.044715) * square)
    ext2[0, 1:3] = act.reshape(2, 4, 32, 256)

    for c in first[1]:
        c.wait_recv()
    spread(banda, ext1, 1, t_ref)

    def put_grad(ch, row, value):
        value = value.astype(BF)
        gs[ch, 0, row : row + 256] = value[:, :128]
        gs[ch, 1, row : row + 256] = value[:, 128:]

    cores = [
        copy_to(gs.at[ch, 1 - core], crecv.at[ch], sc.at[ch], rc.at[ch], partner) for ch in range(2)
    ]
    for k in range(3):
        put_grad(0, k * 256, dot(t_ref[k], act, 0, 0))
    cores[0].start()
    act_grad = mixed(t_ref, w2_ref, 0).astype(BF).astype(F32)
    hid_grad = (act_grad * slope[...]).astype(BF)
    ext2[1, 1:3] = hid_grad.reshape(2, 4, 32, 256)
    for k in range(3):
        put_grad(1, k * 256, dot(hid_grad, u_ref[k], 0, 0))
    cores[1].start()
    pl.semaphore_wait(tok.at[1], 4)
    for d in (2, 14):
        signal(tok.at[2], z_device((z + d) % 16))

    def piece(ch, s):
        peer, device = xy_peer(s)
        rows = pl.ds(pl.multiple_of(peer * PIECE, 16), PIECE)
        return copy_to(xs.at[ch, rows], xrecv.at[ch, s - 1], sx.at[ch, s - 1], rx.at[ch, s - 1], device)

    for ch in range(2):
        cores[ch].wait_recv()
        xs[ch] = (gs[ch, core].astype(F32) + crecv[ch].astype(F32)).astype(BF)

        def send_piece(s, c, ch=ch):
            piece(ch, far_first(s)).start()
            return c

        lax.fori_loop(0, 15, send_piece, 0)

    pl.semaphore_wait(tok.at[2], 2)
    for d in (4, 12):
        signal(tok.at[3], z_device((z + d) % 16))

    mine = pl.ds(pl.multiple_of(me * PIECE, 16), PIECE)

    def near(ch, s):
        return copy_to(zrecv.at[ch, p], zrecv.at[ch, p], sz.at[ch, s - 1], rz.at[ch, p], z_device(grp * 4 + (p + s) % 4))

    def near_in(ch, s):
        q = (p + s) % 4
        return copy_to(zrecv.at[ch, q], zrecv.at[ch, q], sz.at[ch, s - 1], rz.at[ch, q], z_device(grp * 4 + q))

    for ch in range(2):

        def add_piece(s, total, ch=ch):
            piece(ch, s).wait_recv()
            return total + xrecv[ch, s - 1].astype(F32)

        zrecv[ch, p] = lax.fori_loop(1, 16, add_piece, xs[ch, mine].astype(F32)).astype(BF)
        for s in range(1, 4):
            near(ch, s).start()

    second = [c for f in range(2) for c in rows(ext2, f, s2, r2, 8 * f) + edges(ext2, f, s2, r2, 8 * f + 2)]
    for c in second:
        c.start()

    def far(ch, n, group, member):
        return copy_to(
            zgroup.at[ch, grp], zgroup.at[ch, grp], sf.at[ch, n], rf.at[ch, grp], z_device(group * 4 + member)
        )

    before, after, opposite = (grp + 3) % 4, (grp + 1) % 4, (grp + 2) % 4
    to_left = [(opposite, 2), (opposite, 3), (before, 0), (before, 1), (before, 2), (before, 3)]
    to_right = [(opposite, 1), (opposite, 0), (after, 3), (after, 2), (after, 1), (after, 0)]

    def all_four(ref):
        total = ref[0].astype(F32)
        for q in range(1, 4):
            total = total + ref[q].astype(F32)
        return total.astype(BF)

    pl.semaphore_wait(tok.at[3], 2)
    for ch in range(2):
        for s in range(1, 4):
            near_in(ch, s).wait_recv()
        zgroup[ch, grp] = all_four(zrecv.at[ch])

        @pl.when(p == 0)
        def _(ch=ch):
            for n in range(6):
                far(ch, n, *to_left[n]).start()

        @pl.when(p == 3)
        def _(ch=ch):
            for n in range(6):
                far(ch, n, *to_right[n]).start()

    def spread_piece(ch, s):
        cells = fin.at[ch, core, mine]
        return copy_to(cells, cells, sa.at[ch, s - 1], ra.at[ch, s - 1], xy_peer(s)[1])

    for ch in range(2):
        for s in range(1, 4):
            q = (grp + s) % 4
            cells = zgroup.at[ch, q]
            copy_to(cells, cells, sf.at[ch, 0], rf.at[ch, q], z_device(q * 4)).wait_recv()
        fin[ch, core, mine] = all_four(zgroup.at[ch])

        def send_back(s, c, ch=ch):
            spread_piece(ch, far_first(s)).start()
            return c

        lax.fori_loop(0, 15, send_back, 0)

    def turned_back(cells, out):
        for h in range(2):
            lanes = slice(h * 128, h * 128 + 128)
            both = jnp.concatenate([cells[0:128, lanes], cells[128:256, lanes]], axis=1)
            out[h * 256 : h * 256 + 256] = dot(sel[...], both, 1, 1).astype(BF)

    for c in second:
        c.wait_recv()
    spread(bandf, ext2, 0, u_ref)
    turned_back(mixed(u_ref, w2_ref, 1).astype(BF), lo_ref)
    spread(banda, ext2, 1, t_ref)
    turned_back(mixed(t_ref, w1_ref, 0).astype(BF), sg_ref)

    for c in first[0] + first[1] + first[2] + second + cores:
        c.wait_send()
    for ch in range(2):

        def wait_sent(s, c, ch=ch):
            piece(ch, s).wait_send()
            return c

        lax.fori_loop(1, 16, wait_sent, 0)
        for s in range(1, 4):
            near(ch, s).wait_send()

        @pl.when(p == 0)
        def _(ch=ch):
            for n in range(6):
                far(ch, n, *to_left[n]).wait_send()

        @pl.when(p == 3)
        def _(ch=ch):
            for n in range(6):
                far(ch, n, *to_right[n]).wait_send()

    swaps = [copy_to(fin.at[ch, core], fin.at[ch, core], sd.at[ch], rd.at[ch], partner) for ch in range(2)]
    for ch in range(2):

        def wait_back(s, c, ch=ch):
            spread_piece(ch, s).wait()
            return c

        lax.fori_loop(1, 16, wait_back, 0)
        swaps[ch].start()
    for c in swaps:
        c.wait()


def finish(lo_ref, sg_ref, fin, lo_hbm, sg_hbm, d1_hbm, d2_hbm, d_ref, sems):
    stores = [
        pltpu.make_async_copy(lo_ref, lo_hbm, sems.at[6]),
        pltpu.make_async_copy(sg_ref, sg_hbm, sems.at[7]),
    ]
    scale = 1.0 / math.sqrt(4 * 64 * 512)
    for n in range(2):
        for k in range(3):
            for h in range(2):
                rows = slice(k * 256, k * 256 + 256)
                d_ref[n, k, :, h * 128 : h * 128 + 128] = fin[n, h, rows].astype(F32) * scale
            stores.append(pltpu.make_async_copy(d_ref.at[n, k], (d2_hbm, d1_hbm)[n].at[k], sems.at[3 * n + k]))
            stores[-1].start()
    stores[0].start()
    stores[1].start()
    for c in stores:
        c.wait()


def body(state_field, first_weight, second_weight, quadrature, lat_offsets, lon_offsets, cotangent):
    vmem = pl.BlockSpec(memory_space=pltpu.VMEM)
    anywhere = pl.BlockSpec(memory_space=pl.ANY)
    dma = pltpu.SemaphoreType.DMA
    lo, sg, fin = pl.pallas_call(
        kernel,
        out_shape=(
            pltpu.VMEM((512, 128), BF),
            pltpu.VMEM((512, 128), BF),
            pltpu.VMEM((2, 2, 768, 128), BF),
        ),
        in_specs=[anywhere] * 7,
        out_specs=[vmem] * 3,
        scratch_shapes=[
            pltpu.VMEM((2, 512, 128), BF),
            pltpu.VMEM((3, 256, 256), BF),
            pltpu.VMEM((3, 256, 256), BF),
            pltpu.VMEM((3, 2, 12), F32),
            pltpu.VMEM((3, 2, 12), jnp.int32),
            pltpu.VMEM((3, 2, 12), jnp.int32),
            pltpu.VMEM((256, 256), BF),
            pltpu.VMEM((2, 5, 4, 32, 256), BF),
            pltpu.VMEM((2, 5, 4, 32, 256), BF),
            pltpu.VMEM((8, 128), F32),
            pltpu.VMEM((2, 8, 128), F32),
            pltpu.VMEM((2, 384, 512), BF),
            pltpu.VMEM((2, 384, 512), BF),
            pltpu.VMEM((3, 256, 256), BF),
            pltpu.VMEM((3, 256, 256), BF),
            pltpu.VMEM((256, 256), F32),
            pltpu.VMEM((2, 2, 768, 128), BF),
            pltpu.VMEM((2, 768, 128), BF),
            pltpu.VMEM((2, 768, 128), BF),
            pltpu.VMEM((2, 15, PIECE, 128), BF),
            pltpu.VMEM((2, 4, PIECE, 128), BF),
            pltpu.VMEM((2, 4, PIECE, 128), BF),
            dma((7,)),
            dma((18,)), dma((18,)),
            dma((16,)), dma((16,)),
            dma((2,)), dma((2,)),
            dma((2, 15)), dma((2, 15)),
            dma((2, 3)), dma((2, 4)),
            dma((2, 6)), dma((2, 4)),
            dma((2, 15)), dma((2, 15)),
            dma((2,)), dma((2,)),
            pltpu.SemaphoreType.REGULAR((4,)),
        ],
        compiler_params=pltpu.CompilerParams(collective_id=0, has_side_effects=True, vmem_limit_bytes=60 * 2**20),
        cost_estimate=pl.CostEstimate(flops=1_500_000_000, bytes_accessed=4_000_000, transcendentals=65536),
        name="conv_pair",
    )(
        state_field.reshape(512, 128),
        cotangent.reshape(512, 128),
        first_weight,
        second_weight,
        *(jnp.transpose(t, (1, 0, 2)) for t in (quadrature, lat_offsets, lon_offsets)),
    )
    lo, sg, d1, d2 = pl.pallas_call(
        finish,
        out_shape=(
            jax.ShapeDtypeStruct((512, 128), BF),
            jax.ShapeDtypeStruct((512, 128), BF),
            jax.ShapeDtypeStruct((3, 256, 256), F32),
            jax.ShapeDtypeStruct((3, 256, 256), F32),
        ),
        in_specs=[vmem] * 3,
        out_specs=[anywhere] * 4,
        scratch_shapes=[pltpu.VMEM((2, 3, 256, 256), F32), dma((8,))],
        compiler_params=pltpu.CompilerParams(vmem_limit_bytes=4 * 2**20),
        name="put_out",
    )(lo, sg, fin)
    return lo.reshape(1, 256, 2, 128), sg.reshape(1, 256, 2, 128), d1, d2


def solution(mesh):
    in_specs = (
        P("ens", None, "lat", "lon"),
        P(),
        P(),
        P("lat", None, None),
        P("lat", None, None),
        P("lat", None, None),
        P("ens", None, "lat", "lon"),
    )
    out_specs = (P("ens", None, "lat", "lon"), P("ens", None, "lat", "lon"), P(), P())
    return jax.shard_map(body, mesh=mesh, in_specs=in_specs, out_specs=out_specs, check_vma=False)
```

```python
import math

import jax
import jax.numpy as jnp
from jax import lax
from jax.experimental import pallas as pl
from jax.experimental.pallas import tpu as pltpu
from jax.sharding import PartitionSpec as P

MESH = pl.DeviceIdType.MESH
BF = jnp.bfloat16
F32 = jnp.float32

PIECE = 48


def dot(a, b, ca, cb):
    return lax.dot_general(a, b, (((ca,), (cb,)), ((), ())), preferred_element_type=F32)


def copy_to(src, dst, send, recv, device):
    return pltpu.make_async_remote_copy(
        src_ref=src, dst_ref=dst, send_sem=send, recv_sem=recv, device_id=device, device_id_type=MESH
    )


def tap_rows(quad, lat_off, lon_off, sign):
    lane = lax.broadcasted_iota(jnp.int32, (8, 128), 1)
    code = 32 * (lat_off + 1) + sign * lon_off
    code = jnp.where(code < 0, code + 128, code)
    total = jnp.zeros((8, 128), F32)
    for s in range(12):
        total = total + jnp.where(lane == code[:, s : s + 1], quad[:, s : s + 1], 0.0)
    return total.astype(BF).astype(F32)


def one_tap(taps, a):
    lane = lax.broadcasted_iota(jnp.int32, (8, 128), 1)
    moved = taps if a == 0 else pltpu.roll(taps, 128 - 32 * a, 1)
    return jnp.where((lane < 5) | (lane > 123), moved, 0.0)


def banded(row, count, first, shift):
    wide = jnp.broadcast_to(row, (count, 128))
    return pltpu.roll(wide, (shift + first) % 128, 1, stride=1, stride_axis=0)


def put_main(band, i, out, c, row):
    block = banded(row, 128, 0, 0)
    lane = lax.broadcasted_iota(jnp.int32, (16, 128), 1)
    band[i, out : out + 16, c : c + 128] = jnp.where(lane < 64, block[0:16], 0.0).astype(BF)
    band[i, out + 16 : out + 112, c : c + 128] = block[16:112].astype(BF)
    band[i, out + 112 : out + 128, c : c + 128] = jnp.where(lane >= 64, block[112:128], 0.0).astype(BF)


def edge_band(rows_of, first):
    total = jnp.zeros((16, 128), F32)
    lane = lax.broadcasted_iota(jnp.int32, (16, 128), 1)
    for place, row in rows_of:
        t = lane - 32 * place
        block = banded(row, 16, first, 32 * place + 16)
        ok = (t >= 0) & (t < 16) if first == 0 else (t >= 16) & (t < 32)
        total = total + jnp.where(ok, block, 0.0)
    return total.astype(BF)


def kernel(
    x_hbm, g_hbm, w1_hbm, w2_hbm, quad_hbm, lato_hbm, lono_hbm,
    lo_ref, sg_ref, fin,
    xg, w1_ref, w2_ref, quad_ref, lato_ref, lono_ref, sel,
    ext1, ext2, bsend, brecv, bandf, banda, u_ref, t_ref, slope,
    gs, crecv, xs, xrecv, zrecv, zgroup,
    si, s1, r1, s2, r2, sc, rc, sx, rx, sz, rz, sf, rf, sa, ra, sd, rd, tok,
):
    e, l, x = lax.axis_index("ens"), lax.axis_index("lat"), lax.axis_index("lon")
    yh, core = e // 2, e % 2
    z, yl = l // 2, l % 2
    y = yh * 2 + yl
    me = y * 4 + x
    p, grp = z % 4, z // 4
    up, down = (l + 31) % 32, (l + 1) % 32
    left, right = (x + 3) % 4, (x + 1) % 4
    partner = (yh * 2 + 1 - core, l, x)
    across = ((1 - yh) * 2 + core, z * 2 + 1 - yl, x)

    def xy_peer(s):
        xx, yy = (x + s % 4) % 4, (y + s // 4) % 4
        return yy * 4 + xx, ((yy // 2) * 2 + core, z * 2 + yy % 2, xx)

    def far_first(n):
        def pick(i):
            return (2 + i + (i // 2) * (1 + 2 * (i % 2))) % 4

        return 4 * pick(n // 4) + pick(n % 4)

    def z_device(zz):
        return (e, zz * 2 + yl, x)

    loads = [
        pltpu.make_async_copy(src, dst, si.at[n])
        for n, (src, dst) in enumerate(
            (
                (x_hbm, xg.at[0]), (quad_hbm, quad_ref), (lato_hbm, lato_ref), (lono_hbm, lono_ref),
                (g_hbm, xg.at[1]), (w1_hbm, w1_ref), (w2_hbm, w2_ref),
            )
        )
    ]
    for n in (1, 2, 3, 0, 4, 5, 6):
        loads[n].start()

    barrier = pltpu.get_barrier_semaphore()

    def signal(sem, device):
        pl.semaphore_signal(sem, inc=1, device_id=device, device_id_type=MESH)

    for ll, xx in ((up, x), (down, x), (l, left), (l, right), (up, left), (up, right), (down, left), (down, right)):
        signal(barrier, (e, ll, xx))
    signal(barrier, partner)
    signal(barrier, across)

    at = lax.broadcasted_iota(jnp.int32, (256, 256), 0)
    to = lax.broadcasted_iota(jnp.int32, (256, 256), 1)
    sel[...] = jnp.where(at == jnp.where(to < 128, 2 * to, 2 * to - 255), 1.0, 0.0).astype(BF)

    def turn(f):
        for h in range(2):
            got = dot(xg[f, h * 256 : h * 256 + 256], sel[...], 0, 0).astype(BF)
            for r in range(2):
                ext1[f, 1 + r, :, :, h * 128 : h * 128 + 128] = got[:, r * 128 : r * 128 + 128].reshape(4, 32, 128)

    def rows(ext, f, s, r, n):
        return [
            copy_to(ext.at[f, 1], ext.at[f, 4], s.at[n], r.at[n], (e, up, x)),
            copy_to(ext.at[f, 2], ext.at[f, 0], s.at[n + 1], r.at[n + 1], (e, down, x)),
        ]

    def edges(ext, f, s, r, n):
        return [
            copy_to(ext.at[f, 2, 3, 16:32], ext.at[f, 3, 0, 0:16], s.at[n], r.at[n], (e, down, right)),
            copy_to(ext.at[f, 2, 0, 0:16], ext.at[f, 3, 0, 16:32], s.at[n + 1], r.at[n + 1], (e, down, left)),
            copy_to(ext.at[f, 1, 3, 16:32], ext.at[f, 3, 3, 0:16], s.at[n + 2], r.at[n + 2], (e, up, right)),
            copy_to(ext.at[f, 1, 0, 0:16], ext.at[f, 3, 3, 16:32], s.at[n + 3], r.at[n + 3], (e, up, left)),
            copy_to(ext.at[f, 1:3, 3, 16:32], ext.at[f, 3, 1:3, 0:16], s.at[n + 4], r.at[n + 4], (e, l, right)),
            copy_to(ext.at[f, 1:3, 0, 0:16], ext.at[f, 3, 1:3, 16:32], s.at[n + 5], r.at[n + 5], (e, l, left)),
        ]

    first = [edges(ext1, f, s1, r1, 8 * f) + rows(ext1, f, s1, r1, 8 * f + 6) for f in range(2)]
    first.append(
        [
            copy_to(bsend, brecv.at[1], s1.at[16], r1.at[16], (e, up, x)),
            copy_to(bsend, brecv.at[0], s1.at[17], r1.at[17], (e, down, x)),
        ]
    )
    for n in (1, 2, 3):
        loads[n].wait()
    pad = jnp.zeros((2, 12), jnp.int32)
    lato = jnp.concatenate([lato_ref[:, 0], lato_ref[:, 1], pad])
    lono = jnp.concatenate([lono_ref[:, 0], lono_ref[:, 1], pad])
    quad = jnp.concatenate([quad_ref[:, 0], quad_ref[:, 1], pad.astype(F32)])
    adjoint = tap_rows(quad, lato, lono, -1)
    bsend[...] = adjoint
    loads[0].wait()
    turn(0)
    pl.semaphore_wait(barrier, 10)
    for c in first[2]:
        c.start()
    for c in first[0]:
        c.start()
    loads[4].wait()
    turn(1)
    for c in first[1]:
        c.start()
    for device in ((e, up, x), (e, down, x), (e, l, left), (e, l, right), across):
        signal(tok.at[0], device)

    top, bottom = (l > 0).astype(F32), (l < 31).astype(F32)
    col = ((0, 1, 2, 3), (0, 1, 3, 2))

    def put_bands(band, i, rows):
        for k in range(3):
            for n in range(3):
                put_main(band, i, k * 128, col[i][n] * 128, rows[n](k))
            c = col[i][3] * 128
            places = [(i + n, rows[n](k)) for n in range(3)]
            band[i, k * 128 : k * 128 + 16, c : c + 128] = edge_band(places, 0)
            band[i, k * 128 + 16 : k * 128 + 112, c : c + 128] = jnp.zeros((96, 128), BF)
            band[i, k * 128 + 112 : k * 128 + 128, c : c + 128] = edge_band(places, 112)

    def of(taps, i):
        return lambda k: taps[3 * i + k : 3 * i + k + 1]

    taps = tap_rows(quad, lato, lono, 1)
    fwd = [one_tap(taps, a) for a in range(3)]
    put_bands(bandf, 0, [of(fwd[0] * top, 0), of(fwd[1], 0), of(fwd[2], 0)])
    put_bands(bandf, 1, [of(fwd[0], 1), of(fwd[1], 1), of(fwd[2] * bottom, 1)])
    pl.semaphore_wait(tok.at[0], 5)
    two = (e, l, (x + 2) % 4), ((1 - yh) * 2 + core, l, x), z_device((z + 1) % 16), z_device((z + 15) % 16)
    for device in two:
        signal(tok.at[1], device)
    for c in first[2]:
        c.wait_recv()
    adj = [one_tap(adjoint, a) for a in range(3)]
    put_bands(banda, 0, [of(one_tap(brecv[0], 2) * top, 1), of(adj[1], 0), of(adj[0], 1)])
    put_bands(banda, 1, [of(adj[2], 0), of(adj[1], 1), of(one_tap(brecv[1], 0) * bottom, 0)])

    def spread(band, ext, f, out):
        for i in range(2):
            cells = ext[f, i : i + 4].reshape(512, 256)
            got = dot(band[i], cells, 1, 0).astype(BF)
            for k in range(3):
                out[k, i * 128 : i * 128 + 128] = got[k * 128 : k * 128 + 128]

    def mixed(spreaded, weight, cw):
        total = dot(spreaded[0], weight[0], 1, cw)
        for k in range(1, 3):
            total = total + dot(spreaded[k], weight[k], 1, cw)
        return total

    loads[5].wait()
    loads[6].wait()
    for c in first[0]:
        c.wait_recv()
    spread(bandf, ext1, 0, u_ref)
    hidden = mixed(u_ref, w1_ref, 1)
    root = math.sqrt(2.0 / math.pi)
    square = hidden * hidden
    bend = jnp.tanh(root * hidden * (1.0 + 0.044715 * square))
    act = (0.5 * hidden * (1.0 + bend)).astype(BF)
    slope[...] = 0.5 * (1.0 + bend) + (0.5 * root) * hidden * (1.0 - bend * bend) * (1.0 + (3 * 0.044715) * square)
    ext2[0, 1:3] = act.reshape(2, 4, 32, 256)

    pl.semaphore_wait(tok.at[1], 4)
    for d in (2, 14):
        signal(tok.at[2], z_device((z + d) % 16))
    for c in first[1]:
        c.wait_recv()
    spread(banda, ext1, 1, t_ref)

    def put_grad(ch, row, value):
        value = value.astype(BF)
        gs[ch, 0, row : row + 256] = value[:, :128]
        gs[ch, 1, row : row + 256] = value[:, 128:]

    cores = [
        copy_to(gs.at[ch, 1 - core], crecv.at[ch], sc.at[ch], rc.at[ch], partner) for ch in range(2)
    ]
    for k in range(3):
        put_grad(0, k * 256, dot(t_ref[k], act, 0, 0))
    cores[0].start()
    act_grad = mixed(t_ref, w2_ref, 0).astype(BF).astype(F32)
    hid_grad = (act_grad * slope[...]).astype(BF)
    ext2[1, 1:3] = hid_grad.reshape(2, 4, 32, 256)
    for k in range(3):
        put_grad(1, k * 256, dot(hid_grad, u_ref[k], 0, 0))
    cores[1].start()
    pl.semaphore_wait(tok.at[2], 2)
    for d in (4, 12):
        signal(tok.at[3], z_device((z + d) % 16))

    def piece(ch, s):
        peer, device = xy_peer(s)
        rows = pl.ds(pl.multiple_of(peer * PIECE, 16), PIECE)
        return copy_to(xs.at[ch, rows], xrecv.at[ch, s - 1], sx.at[ch, s - 1], rx.at[ch, s - 1], device)

    for ch in range(2):
        cores[ch].wait_recv()
        xs[ch] = (gs[ch, core].astype(F32) + crecv[ch].astype(F32)).astype(BF)

        def send_piece(s, c, ch=ch):
            piece(ch, far_first(s)).start()
            return c

        lax.fori_loop(0, 15, send_piece, 0)

    mine = pl.ds(pl.multiple_of(me * PIECE, 16), PIECE)

    def near(ch, s):
        return copy_to(zrecv.at[ch, p], zrecv.at[ch, p], sz.at[ch, s - 1], rz.at[ch, p], z_device(grp * 4 + (p + s) % 4))

    def near_in(ch, s):
        q = (p + s) % 4
        return copy_to(zrecv.at[ch, q], zrecv.at[ch, q], sz.at[ch, s - 1], rz.at[ch, q], z_device(grp * 4 + q))

    for ch in range(2):

        def add_piece(s, total, ch=ch):
            piece(ch, s).wait_recv()
            return total + xrecv[ch, s - 1].astype(F32)

        zrecv[ch, p] = lax.fori_loop(1, 16, add_piece, xs[ch, mine].astype(F32)).astype(BF)
        for s in range(1, 4):
            near(ch, s).start()

    second = [c for f in range(2) for c in rows(ext2, f, s2, r2, 8 * f) + edges(ext2, f, s2, r2, 8 * f + 2)]

    def far(ch, n, group, member):
        return copy_to(
            zgroup.at[ch, grp], zgroup.at[ch, grp], sf.at[ch, n], rf.at[ch, grp], z_device(group * 4 + member)
        )

    before, after, opposite = (grp + 3) % 4, (grp + 1) % 4, (grp + 2) % 4
    to_left = [(opposite, 2), (opposite, 3), (before, 0), (before, 1), (before, 2), (before, 3)]
    to_right = [(opposite, 1), (opposite, 0), (after, 3), (after, 2), (after, 1), (after, 0)]

    def all_four(ref):
        total = ref[0].astype(F32)
        for q in range(1, 4):
            total = total + ref[q].astype(F32)
        return total.astype(BF)

    pl.semaphore_wait(tok.at[3], 2)
    for ch in range(2):
        for s in range(1, 4):
            near_in(ch, s).wait_recv()
        zgroup[ch, grp] = all_four(zrecv.at[ch])

        @pl.when(p == 0)
        def _(ch=ch):
            for n in range(6):
                far(ch, n, *to_left[n]).start()

        @pl.when(p == 3)
        def _(ch=ch):
            for n in range(6):
                far(ch, n, *to_right[n]).start()

    for c in second:
        c.start()

    def spread_piece(ch, s):
        cells = fin.at[ch, core, mine]
        return copy_to(cells, cells, sa.at[ch, s - 1], ra.at[ch, s - 1], xy_peer(s)[1])

    for ch in range(2):
        for s in range(1, 4):
            q = (grp + s) % 4
            cells = zgroup.at[ch, q]
            copy_to(cells, cells, sf.at[ch, 0], rf.at[ch, q], z_device(q * 4)).wait_recv()
        fin[ch, core, mine] = all_four(zgroup.at[ch])

        def send_back(s, c, ch=ch):
            spread_piece(ch, far_first(s)).start()
            return c

        lax.fori_loop(0, 15, send_back, 0)

    def turned_back(cells, out):
        for h in range(2):
            lanes = slice(h * 128, h * 128 + 128)
            both = jnp.concatenate([cells[0:128, lanes], cells[128:256, lanes]], axis=1)
            out[h * 256 : h * 256 + 256] = dot(sel[...], both, 1, 1).astype(BF)

    for c in second:
        c.wait_recv()
    spread(bandf, ext2, 0, u_ref)
    turned_back(mixed(u_ref, w2_ref, 1).astype(BF), lo_ref)
    spread(banda, ext2, 1, t_ref)
    turned_back(mixed(t_ref, w1_ref, 0).astype(BF), sg_ref)

    for c in first[0] + first[1] + first[2] + second + cores:
        c.wait_send()
    for ch in range(2):

        def wait_sent(s, c, ch=ch):
            piece(ch, s).wait_send()
            return c

        lax.fori_loop(1, 16, wait_sent, 0)
        for s in range(1, 4):
            near(ch, s).wait_send()

        @pl.when(p == 0)
        def _(ch=ch):
            for n in range(6):
                far(ch, n, *to_left[n]).wait_send()

        @pl.when(p == 3)
        def _(ch=ch):
            for n in range(6):
                far(ch, n, *to_right[n]).wait_send()

    swaps = [copy_to(fin.at[ch, core], fin.at[ch, core], sd.at[ch], rd.at[ch], partner) for ch in range(2)]
    for ch in range(2):

        def wait_back(s, c, ch=ch):
            spread_piece(ch, s).wait()
            return c

        lax.fori_loop(1, 16, wait_back, 0)
        swaps[ch].start()
    for c in swaps:
        c.wait()


def finish(lo_ref, sg_ref, fin, lo_hbm, sg_hbm, d1_hbm, d2_hbm, d_ref, sems):
    stores = [
        pltpu.make_async_copy(lo_ref, lo_hbm, sems.at[6]),
        pltpu.make_async_copy(sg_ref, sg_hbm, sems.at[7]),
    ]
    scale = 1.0 / math.sqrt(4 * 64 * 512)
    for n in range(2):
        for k in range(3):
            for h in range(2):
                rows = slice(k * 256, k * 256 + 256)
                d_ref[n, k, :, h * 128 : h * 128 + 128] = fin[n, h, rows].astype(F32) * scale
            stores.append(pltpu.make_async_copy(d_ref.at[n, k], (d2_hbm, d1_hbm)[n].at[k], sems.at[3 * n + k]))
            stores[-1].start()
    stores[0].start()
    stores[1].start()
    for c in stores:
        c.wait()


def body(state_field, first_weight, second_weight, quadrature, lat_offsets, lon_offsets, cotangent):
    vmem = pl.BlockSpec(memory_space=pltpu.VMEM)
    anywhere = pl.BlockSpec(memory_space=pl.ANY)
    dma = pltpu.SemaphoreType.DMA
    lo, sg, fin = pl.pallas_call(
        kernel,
        out_shape=(
            pltpu.VMEM((512, 128), BF),
            pltpu.VMEM((512, 128), BF),
            pltpu.VMEM((2, 2, 768, 128), BF),
        ),
        in_specs=[anywhere] * 7,
        out_specs=[vmem] * 3,
        scratch_shapes=[
            pltpu.VMEM((2, 512, 128), BF),
            pltpu.VMEM((3, 256, 256), BF),
            pltpu.VMEM((3, 256, 256), BF),
            pltpu.VMEM((3, 2, 12), F32),
            pltpu.VMEM((3, 2, 12), jnp.int32),
            pltpu.VMEM((3, 2, 12), jnp.int32),
            pltpu.VMEM((256, 256), BF),
            pltpu.VMEM((2, 5, 4, 32, 256), BF),
            pltpu.VMEM((2, 5, 4, 32, 256), BF),
            pltpu.VMEM((8, 128), F32),
            pltpu.VMEM((2, 8, 128), F32),
            pltpu.VMEM((2, 384, 512), BF),
            pltpu.VMEM((2, 384, 512), BF),
            pltpu.VMEM((3, 256, 256), BF),
            pltpu.VMEM((3, 256, 256), BF),
            pltpu.VMEM((256, 256), F32),
            pltpu.VMEM((2, 2, 768, 128), BF),
            pltpu.VMEM((2, 768, 128), BF),
            pltpu.VMEM((2, 768, 128), BF),
            pltpu.VMEM((2, 15, PIECE, 128), BF),
            pltpu.VMEM((2, 4, PIECE, 128), BF),
            pltpu.VMEM((2, 4, PIECE, 128), BF),
            dma((7,)),
            dma((18,)), dma((18,)),
            dma((16,)), dma((16,)),
            dma((2,)), dma((2,)),
            dma((2, 15)), dma((2, 15)),
            dma((2, 3)), dma((2, 4)),
            dma((2, 6)), dma((2, 4)),
            dma((2, 15)), dma((2, 15)),
            dma((2,)), dma((2,)),
            pltpu.SemaphoreType.REGULAR((4,)),
        ],
        compiler_params=pltpu.CompilerParams(collective_id=0, has_side_effects=True, vmem_limit_bytes=60 * 2**20),
        cost_estimate=pl.CostEstimate(flops=1_500_000_000, bytes_accessed=4_000_000, transcendentals=65536),
        name="conv_pair",
    )(
        state_field.reshape(512, 128),
        cotangent.reshape(512, 128),
        first_weight,
        second_weight,
        *(jnp.transpose(t, (1, 0, 2)) for t in (quadrature, lat_offsets, lon_offsets)),
    )
    lo, sg, d1, d2 = pl.pallas_call(
        finish,
        out_shape=(
            jax.ShapeDtypeStruct((512, 128), BF),
            jax.ShapeDtypeStruct((512, 128), BF),
            jax.ShapeDtypeStruct((3, 256, 256), F32),
            jax.ShapeDtypeStruct((3, 256, 256), F32),
        ),
        in_specs=[vmem] * 3,
        out_specs=[anywhere] * 4,
        scratch_shapes=[pltpu.VMEM((2, 3, 256, 256), F32), dma((8,))],
        compiler_params=pltpu.CompilerParams(vmem_limit_bytes=4 * 2**20),
        name="put_out",
    )(lo, sg, fin)
    return lo.reshape(1, 256, 2, 128), sg.reshape(1, 256, 2, 128), d1, d2


def solution(mesh):
    in_specs = (
        P("ens", None, "lat", "lon"),
        P(),
        P(),
        P("lat", None, None),
        P("lat", None, None),
        P("lat", None, None),
        P("ens", None, "lat", "lon"),
    )
    out_specs = (P("ens", None, "lat", "lon"), P("ens", None, "lat", "lon"), P(), P())
    return jax.shard_map(body, mesh=mesh, in_specs=in_specs, out_specs=out_specs, check_vma=False)
```

```python
import math

import jax
import jax.numpy as jnp
from jax import lax
from jax.experimental import pallas as pl
from jax.experimental.pallas import tpu as pltpu
from jax.sharding import PartitionSpec as P

MESH = pl.DeviceIdType.MESH
BF = jnp.bfloat16
F32 = jnp.float32

PIECE = 48


def dot(a, b, ca, cb):
    return lax.dot_general(a, b, (((ca,), (cb,)), ((), ())), preferred_element_type=F32)


def copy_to(src, dst, send, recv, device):
    return pltpu.make_async_remote_copy(
        src_ref=src, dst_ref=dst, send_sem=send, recv_sem=recv, device_id=device, device_id_type=MESH
    )


def tap_rows(quad, lat_off, lon_off, sign):
    lane = lax.broadcasted_iota(jnp.int32, (8, 128), 1)
    code = 32 * (lat_off + 1) + sign * lon_off
    code = jnp.where(code < 0, code + 128, code)
    total = jnp.zeros((8, 128), F32)
    for s in range(12):
        total = total + jnp.where(lane == code[:, s : s + 1], quad[:, s : s + 1], 0.0)
    return total.astype(BF).astype(F32)


def one_tap(taps, a):
    lane = lax.broadcasted_iota(jnp.int32, (8, 128), 1)
    moved = taps if a == 0 else pltpu.roll(taps, 128 - 32 * a, 1)
    return jnp.where((lane < 5) | (lane > 123), moved, 0.0)


def banded(row, count, first, shift):
    wide = jnp.broadcast_to(row, (count, 128))
    return pltpu.roll(wide, (shift + first) % 128, 1, stride=1, stride_axis=0)


def put_main(band, i, out, c, row):
    block = banded(row, 128, 0, 0)
    lane = lax.broadcasted_iota(jnp.int32, (16, 128), 1)
    band[i, out : out + 16, c : c + 128] = jnp.where(lane < 64, block[0:16], 0.0).astype(BF)
    band[i, out + 16 : out + 112, c : c + 128] = block[16:112].astype(BF)
    band[i, out + 112 : out + 128, c : c + 128] = jnp.where(lane >= 64, block[112:128], 0.0).astype(BF)


def edge_band(rows_of, first):
    total = jnp.zeros((16, 128), F32)
    lane = lax.broadcasted_iota(jnp.int32, (16, 128), 1)
    for place, row in rows_of:
        t = lane - 32 * place
        block = banded(row, 16, first, 32 * place + 16)
        ok = (t >= 0) & (t < 16) if first == 0 else (t >= 16) & (t < 32)
        total = total + jnp.where(ok, block, 0.0)
    return total.astype(BF)


def kernel(
    x_hbm, g_hbm, w1_hbm, w2_hbm, quad_hbm, lato_hbm, lono_hbm,
    lo_ref, sg_ref, fin,
    xg, w1_ref, w2_ref, quad_ref, lato_ref, lono_ref, sel,
    ext1, ext2, bsend, brecv, bandf, banda, u_ref, t_ref, slope,
    gs, crecv, xs, xrecv, zrecv, zgroup,
    si, s1, r1, s2, r2, sc, rc, sx, rx, sz, rz, sf, rf, sa, ra, sd, rd, tok,
):
    e, l, x = lax.axis_index("ens"), lax.axis_index("lat"), lax.axis_index("lon")
    yh, core = e // 2, e % 2
    z, yl = l // 2, l % 2
    y = yh * 2 + yl
    me = y * 4 + x
    p, grp = z % 4, z // 4
    up, down = (l + 31) % 32, (l + 1) % 32
    left, right = (x + 3) % 4, (x + 1) % 4
    partner = (yh * 2 + 1 - core, l, x)
    across = ((1 - yh) * 2 + core, z * 2 + 1 - yl, x)

    def xy_peer(s):
        xx, yy = (x + s % 4) % 4, (y + s // 4) % 4
        return yy * 4 + xx, ((yy // 2) * 2 + core, z * 2 + yy % 2, xx)

    def far_first(n):
        def pick(i):
            return (2 + i + (i // 2) * (1 + 2 * (i % 2))) % 4

        return 4 * pick(n // 4) + pick(n % 4)

    def z_device(zz):
        return (e, zz * 2 + yl, x)

    loads = [
        pltpu.make_async_copy(src, dst, si.at[n])
        for n, (src, dst) in enumerate(
            (
                (x_hbm, xg.at[0]), (quad_hbm, quad_ref), (lato_hbm, lato_ref), (lono_hbm, lono_ref),
                (g_hbm, xg.at[1]), (w1_hbm, w1_ref), (w2_hbm, w2_ref),
            )
        )
    ]
    for n in (1, 2, 3, 0, 4, 5, 6):
        loads[n].start()

    barrier = pltpu.get_barrier_semaphore()

    def signal(sem, device):
        pl.semaphore_signal(sem, inc=1, device_id=device, device_id_type=MESH)

    for ll, xx in ((up, x), (down, x), (l, left), (l, right), (up, left), (up, right), (down, left), (down, right)):
        signal(barrier, (e, ll, xx))
    signal(barrier, partner)
    signal(barrier, across)

    at = lax.broadcasted_iota(jnp.int32, (256, 256), 0)
    to = lax.broadcasted_iota(jnp.int32, (256, 256), 1)
    sel[...] = jnp.where(at == jnp.where(to < 128, 2 * to, 2 * to - 255), 1.0, 0.0).astype(BF)

    def turn(f):
        for h in range(2):
            got = dot(xg[f, h * 256 : h * 256 + 256], sel[...], 0, 0).astype(BF)
            for r in range(2):
                ext1[f, 1 + r, :, :, h * 128 : h * 128 + 128] = got[:, r * 128 : r * 128 + 128].reshape(4, 32, 128)

    def rows(ext, f, s, r, n):
        return [
            copy_to(ext.at[f, 1], ext.at[f, 4], s.at[n], r.at[n], (e, up, x)),
            copy_to(ext.at[f, 2], ext.at[f, 0], s.at[n + 1], r.at[n + 1], (e, down, x)),
        ]

    def edges(ext, f, s, r, n):
        return [
            copy_to(ext.at[f, 2, 3, 16:32], ext.at[f, 3, 0, 0:16], s.at[n], r.at[n], (e, down, right)),
            copy_to(ext.at[f, 2, 0, 0:16], ext.at[f, 3, 0, 16:32], s.at[n + 1], r.at[n + 1], (e, down, left)),
            copy_to(ext.at[f, 1, 3, 16:32], ext.at[f, 3, 3, 0:16], s.at[n + 2], r.at[n + 2], (e, up, right)),
            copy_to(ext.at[f, 1, 0, 0:16], ext.at[f, 3, 3, 16:32], s.at[n + 3], r.at[n + 3], (e, up, left)),
            copy_to(ext.at[f, 1:3, 3, 16:32], ext.at[f, 3, 1:3, 0:16], s.at[n + 4], r.at[n + 4], (e, l, right)),
            copy_to(ext.at[f, 1:3, 0, 0:16], ext.at[f, 3, 1:3, 16:32], s.at[n + 5], r.at[n + 5], (e, l, left)),
        ]

    first = [edges(ext1, f, s1, r1, 8 * f) + rows(ext1, f, s1, r1, 8 * f + 6) for f in range(2)]
    first.append(
        [
            copy_to(bsend, brecv.at[1], s1.at[16], r1.at[16], (e, up, x)),
            copy_to(bsend, brecv.at[0], s1.at[17], r1.at[17], (e, down, x)),
        ]
    )
    for n in (1, 2, 3):
        loads[n].wait()
    pad = jnp.zeros((2, 12), jnp.int32)
    lato = jnp.concatenate([lato_ref[:, 0], lato_ref[:, 1], pad])
    lono = jnp.concatenate([lono_ref[:, 0], lono_ref[:, 1], pad])
    quad = jnp.concatenate([quad_ref[:, 0], quad_ref[:, 1], pad.astype(F32)])
    adjoint = tap_rows(quad, lato, lono, -1)
    bsend[...] = adjoint
    loads[0].wait()
    turn(0)
    pl.semaphore_wait(barrier, 10)
    for c in first[2]:
        c.start()
    for c in first[0]:
        c.start()
    loads[4].wait()
    turn(1)
    for c in first[1]:
        c.start()
    for device in ((e, up, x), (e, down, x), (e, l, left), (e, l, right), across):
        signal(tok.at[0], device)

    top, bottom = (l > 0).astype(F32), (l < 31).astype(F32)
    col = ((0, 1, 2, 3), (0, 1, 3, 2))

    def put_bands(band, i, rows):
        for k in range(3):
            for n in range(3):
                put_main(band, i, k * 128, col[i][n] * 128, rows[n](k))
            c = col[i][3] * 128
            places = [(i + n, rows[n](k)) for n in range(3)]
            band[i, k * 128 : k * 128 + 16, c : c + 128] = edge_band(places, 0)
            band[i, k * 128 + 16 : k * 128 + 112, c : c + 128] = jnp.zeros((96, 128), BF)
            band[i, k * 128 + 112 : k * 128 + 128, c : c + 128] = edge_band(places, 112)

    def of(taps, i):
        return lambda k: taps[3 * i + k : 3 * i + k + 1]

    taps = tap_rows(quad, lato, lono, 1)
    fwd = [one_tap(taps, a) for a in range(3)]
    put_bands(bandf, 0, [of(fwd[0] * top, 0), of(fwd[1], 0), of(fwd[2], 0)])
    put_bands(bandf, 1, [of(fwd[0], 1), of(fwd[1], 1), of(fwd[2] * bottom, 1)])
    pl.semaphore_wait(tok.at[0], 5)
    two = (e, l, (x + 2) % 4), ((1 - yh) * 2 + core, l, x), z_device((z + 1) % 16), z_device((z + 15) % 16)
    for device in two:
        signal(tok.at[1], device)
    for c in first[2]:
        c.wait_recv()
    adj = [one_tap(adjoint, a) for a in range(3)]
    put_bands(banda, 0, [of(one_tap(brecv[0], 2) * top, 1), of(adj[1], 0), of(adj[0], 1)])
    put_bands(banda, 1, [of(adj[2], 0), of(adj[1], 1), of(one_tap(brecv[1], 0) * bottom, 0)])

    def spread(band, ext, f, out):
        for i in range(2):
            cells = ext[f, i : i + 4].reshape(512, 256)
            got = dot(band[i], cells, 1, 0).astype(BF)
            for k in range(3):
                out[k, i * 128 : i * 128 + 128] = got[k * 128 : k * 128 + 128]

    def mixed(spreaded, weight, cw):
        total = dot(spreaded[0], weight[0], 1, cw)
        for k in range(1, 3):
            total = total + dot(spreaded[k], weight[k], 1, cw)
        return total

    loads[5].wait()
    loads[6].wait()
    for c in first[0]:
        c.wait_recv()
    spread(bandf, ext1, 0, u_ref)
    hidden = mixed(u_ref, w1_ref, 1)
    root = math.sqrt(2.0 / math.pi)
    square = hidden * hidden
    bend = jnp.tanh(root * hidden * (1.0 + 0.044715 * square))
    act = (0.5 * hidden * (1.0 + bend)).astype(BF)
    slope[...] = 0.5 * (1.0 + bend) + (0.5 * root) * hidden * (1.0 - bend * bend) * (1.0 + (3 * 0.044715) * square)
    ext2[0, 1:3] = act.reshape(2, 4, 32, 256)

    pl.semaphore_wait(tok.at[1], 4)
    for d in (2, 14):
        signal(tok.at[2], z_device((z + d) % 16))
    for c in first[1]:
        c.wait_recv()
    spread(banda, ext1, 1, t_ref)

    def put_grad(ch, row, value):
        value = value.astype(BF)
        gs[ch, 0, row : row + 256] = value[:, :128]
        gs[ch, 1, row : row + 256] = value[:, 128:]

    cores = [
        copy_to(gs.at[ch, 1 - core], crecv.at[ch], sc.at[ch], rc.at[ch], partner) for ch in range(2)
    ]
    for k in range(3):
        put_grad(0, k * 256, dot(t_ref[k], act, 0, 0))
    cores[0].start()
    act_grad = mixed(t_ref, w2_ref, 0).astype(BF).astype(F32)
    hid_grad = (act_grad * slope[...]).astype(BF)
    ext2[1, 1:3] = hid_grad.reshape(2, 4, 32, 256)
    for k in range(3):
        put_grad(1, k * 256, dot(hid_grad, u_ref[k], 0, 0))
    cores[1].start()
    pl.semaphore_wait(tok.at[2], 2)
    for d in (4, 12):
        signal(tok.at[3], z_device((z + d) % 16))

    def piece(ch, s):
        peer, device = xy_peer(s)
        rows = pl.ds(pl.multiple_of(peer * PIECE, 16), PIECE)
        return copy_to(xs.at[ch, rows], xrecv.at[ch, s - 1], sx.at[ch, s - 1], rx.at[ch, s - 1], device)

    for ch in range(2):
        cores[ch].wait_recv()
        xs[ch] = (gs[ch, core].astype(F32) + crecv[ch].astype(F32)).astype(BF)

        def send_piece(s, c, ch=ch):
            piece(ch, far_first(s)).start()
            return c

        lax.fori_loop(0, 15, send_piece, 0)

    mine = pl.ds(pl.multiple_of(me * PIECE, 16), PIECE)

    def near(ch, s):
        return copy_to(zrecv.at[ch, p], zrecv.at[ch, p], sz.at[ch, s - 1], rz.at[ch, p], z_device(grp * 4 + (p + s) % 4))

    def near_in(ch, s):
        q = (p + s) % 4
        return copy_to(zrecv.at[ch, q], zrecv.at[ch, q], sz.at[ch, s - 1], rz.at[ch, q], z_device(grp * 4 + q))

    for ch in range(2):

        def add_piece(s, total, ch=ch):
            piece(ch, s).wait_recv()
            return total + xrecv[ch, s - 1].astype(F32)

        zrecv[ch, p] = lax.fori_loop(1, 16, add_piece, xs[ch, mine].astype(F32)).astype(BF)
        for s in range(1, 4):
            near(ch, s).start()

    second = [c for f in range(2) for c in rows(ext2, f, s2, r2, 8 * f) + edges(ext2, f, s2, r2, 8 * f + 2)]

    def far(ch, n, group, member):
        return copy_to(
            zgroup.at[ch, grp], zgroup.at[ch, grp], sf.at[ch, n], rf.at[ch, grp], z_device(group * 4 + member)
        )

    before, after, opposite = (grp + 3) % 4, (grp + 1) % 4, (grp + 2) % 4
    to_left = [(opposite, 2), (opposite, 3), (before, 0), (before, 1), (before, 2), (before, 3)]
    to_right = [(opposite, 1), (opposite, 0), (after, 3), (after, 2), (after, 1), (after, 0)]

    def all_four(ref):
        total = ref[0].astype(F32)
        for q in range(1, 4):
            total = total + ref[q].astype(F32)
        return total.astype(BF)

    pl.semaphore_wait(tok.at[3], 2)
    for ch in range(2):
        for s in range(1, 4):
            near_in(ch, s).wait_recv()
        zgroup[ch, grp] = all_four(zrecv.at[ch])

        @pl.when(p == 0)
        def _(ch=ch):
            for n in range(6):
                far(ch, n, *to_left[n]).start()

        @pl.when(p == 3)
        def _(ch=ch):
            for n in range(6):
                far(ch, n, *to_right[n]).start()

    for c in second:
        c.start()

    def spread_piece(ch, s):
        cells = fin.at[ch, core, mine]
        return copy_to(cells, cells, sa.at[ch, s - 1], ra.at[ch, s - 1], xy_peer(s)[1])

    for ch in range(2):
        for s in range(1, 4):
            q = (grp + s) % 4
            cells = zgroup.at[ch, q]
            copy_to(cells, cells, sf.at[ch, 0], rf.at[ch, q], z_device(q * 4)).wait_recv()
        fin[ch, core, mine] = all_four(zgroup.at[ch])

        def send_back(s, c, ch=ch):
            spread_piece(ch, far_first(s)).start()
            return c

        lax.fori_loop(0, 15, send_back, 0)

    swaps = [copy_to(fin.at[ch, core], fin.at[ch, core], sd.at[ch], rd.at[ch], partner) for ch in range(2)]
    for ch in range(2):

        def wait_back(s, c, ch=ch):
            spread_piece(ch, s).wait()
            return c

        lax.fori_loop(1, 16, wait_back, 0)
        swaps[ch].start()

    def turned_back(cells, out):
        for h in range(2):
            lanes = slice(h * 128, h * 128 + 128)
            both = jnp.concatenate([cells[0:128, lanes], cells[128:256, lanes]], axis=1)
            out[h * 256 : h * 256 + 256] = dot(sel[...], both, 1, 1).astype(BF)

    for c in second:
        c.wait_recv()
    spread(bandf, ext2, 0, u_ref)
    turned_back(mixed(u_ref, w2_ref, 1).astype(BF), lo_ref)
    spread(banda, ext2, 1, t_ref)
    turned_back(mixed(t_ref, w1_ref, 0).astype(BF), sg_ref)

    for c in first[0] + first[1] + first[2] + second + cores:
        c.wait_send()
    for ch in range(2):

        def wait_sent(s, c, ch=ch):
            piece(ch, s).wait_send()
            return c

        lax.fori_loop(1, 16, wait_sent, 0)
        for s in range(1, 4):
            near(ch, s).wait_send()

        @pl.when(p == 0)
        def _(ch=ch):
            for n in range(6):
                far(ch, n, *to_left[n]).wait_send()

        @pl.when(p == 3)
        def _(ch=ch):
            for n in range(6):
                far(ch, n, *to_right[n]).wait_send()
    for c in swaps:
        c.wait()


def finish(lo_ref, sg_ref, fin, lo_hbm, sg_hbm, d1_hbm, d2_hbm, d_ref, sems):
    stores = [
        pltpu.make_async_copy(lo_ref, lo_hbm, sems.at[6]),
        pltpu.make_async_copy(sg_ref, sg_hbm, sems.at[7]),
    ]
    scale = 1.0 / math.sqrt(4 * 64 * 512)
    for n in range(2):
        for k in range(3):
            for h in range(2):
                rows = slice(k * 256, k * 256 + 256)
                d_ref[n, k, :, h * 128 : h * 128 + 128] = fin[n, h, rows].astype(F32) * scale
            stores.append(pltpu.make_async_copy(d_ref.at[n, k], (d2_hbm, d1_hbm)[n].at[k], sems.at[3 * n + k]))
            stores[-1].start()
    stores[0].start()
    stores[1].start()
    for c in stores:
        c.wait()


def body(state_field, first_weight, second_weight, quadrature, lat_offsets, lon_offsets, cotangent):
    vmem = pl.BlockSpec(memory_space=pltpu.VMEM)
    anywhere = pl.BlockSpec(memory_space=pl.ANY)
    dma = pltpu.SemaphoreType.DMA
    lo, sg, fin = pl.pallas_call(
        kernel,
        out_shape=(
            pltpu.VMEM((512, 128), BF),
            pltpu.VMEM((512, 128), BF),
            pltpu.VMEM((2, 2, 768, 128), BF),
        ),
        in_specs=[anywhere] * 7,
        out_specs=[vmem] * 3,
        scratch_shapes=[
            pltpu.VMEM((2, 512, 128), BF),
            pltpu.VMEM((3, 256, 256), BF),
            pltpu.VMEM((3, 256, 256), BF),
            pltpu.VMEM((3, 2, 12), F32),
            pltpu.VMEM((3, 2, 12), jnp.int32),
            pltpu.VMEM((3, 2, 12), jnp.int32),
            pltpu.VMEM((256, 256), BF),
            pltpu.VMEM((2, 5, 4, 32, 256), BF),
            pltpu.VMEM((2, 5, 4, 32, 256), BF),
            pltpu.VMEM((8, 128), F32),
            pltpu.VMEM((2, 8, 128), F32),
            pltpu.VMEM((2, 384, 512), BF),
            pltpu.VMEM((2, 384, 512), BF),
            pltpu.VMEM((3, 256, 256), BF),
            pltpu.VMEM((3, 256, 256), BF),
            pltpu.VMEM((256, 256), F32),
            pltpu.VMEM((2, 2, 768, 128), BF),
            pltpu.VMEM((2, 768, 128), BF),
            pltpu.VMEM((2, 768, 128), BF),
            pltpu.VMEM((2, 15, PIECE, 128), BF),
            pltpu.VMEM((2, 4, PIECE, 128), BF),
            pltpu.VMEM((2, 4, PIECE, 128), BF),
            dma((7,)),
            dma((18,)), dma((18,)),
            dma((16,)), dma((16,)),
            dma((2,)), dma((2,)),
            dma((2, 15)), dma((2, 15)),
            dma((2, 3)), dma((2, 4)),
            dma((2, 6)), dma((2, 4)),
            dma((2, 15)), dma((2, 15)),
            dma((2,)), dma((2,)),
            pltpu.SemaphoreType.REGULAR((4,)),
        ],
        compiler_params=pltpu.CompilerParams(collective_id=0, has_side_effects=True, vmem_limit_bytes=60 * 2**20),
        cost_estimate=pl.CostEstimate(flops=1_500_000_000, bytes_accessed=4_000_000, transcendentals=65536),
        name="conv_pair",
    )(
        state_field.reshape(512, 128),
        cotangent.reshape(512, 128),
        first_weight,
        second_weight,
        *(jnp.transpose(t, (1, 0, 2)) for t in (quadrature, lat_offsets, lon_offsets)),
    )
    lo, sg, d1, d2 = pl.pallas_call(
        finish,
        out_shape=(
            jax.ShapeDtypeStruct((512, 128), BF),
            jax.ShapeDtypeStruct((512, 128), BF),
            jax.ShapeDtypeStruct((3, 256, 256), F32),
            jax.ShapeDtypeStruct((3, 256, 256), F32),
        ),
        in_specs=[vmem] * 3,
        out_specs=[anywhere] * 4,
        scratch_shapes=[pltpu.VMEM((2, 3, 256, 256), F32), dma((8,))],
        compiler_params=pltpu.CompilerParams(vmem_limit_bytes=4 * 2**20),
        name="put_out",
    )(lo, sg, fin)
    return lo.reshape(1, 256, 2, 128), sg.reshape(1, 256, 2, 128), d1, d2


def solution(mesh):
    in_specs = (
        P("ens", None, "lat", "lon"),
        P(),
        P(),
        P("lat", None, None),
        P("lat", None, None),
        P("lat", None, None),
        P("ens", None, "lat", "lon"),
    )
    out_specs = (P("ens", None, "lat", "lon"), P("ens", None, "lat", "lon"), P(), P())
    return jax.shard_map(body, mesh=mesh, in_specs=in_specs, out_specs=out_specs, check_vma=False)
```

```python
import math

import jax
import jax.numpy as jnp
from jax import lax
from jax.experimental import pallas as pl
from jax.experimental.pallas import tpu as pltpu
from jax.sharding import PartitionSpec as P

MESH = pl.DeviceIdType.MESH
BF = jnp.bfloat16
F32 = jnp.float32

PIECE = 48


def dot(a, b, ca, cb):
    return lax.dot_general(a, b, (((ca,), (cb,)), ((), ())), preferred_element_type=F32)


def copy_to(src, dst, send, recv, device):
    return pltpu.make_async_remote_copy(
        src_ref=src, dst_ref=dst, send_sem=send, recv_sem=recv, device_id=device, device_id_type=MESH
    )


def tap_rows(quad, lat_off, lon_off, sign):
    lane = lax.broadcasted_iota(jnp.int32, (8, 128), 1)
    code = 32 * (lat_off + 1) + sign * lon_off
    code = jnp.where(code < 0, code + 128, code)
    total = jnp.zeros((8, 128), F32)
    for s in range(12):
        total = total + jnp.where(lane == code[:, s : s + 1], quad[:, s : s + 1], 0.0)
    return total.astype(BF).astype(F32)


def one_tap(taps, a):
    lane = lax.broadcasted_iota(jnp.int32, (8, 128), 1)
    moved = taps if a == 0 else pltpu.roll(taps, 128 - 32 * a, 1)
    return jnp.where((lane < 5) | (lane > 123), moved, 0.0)


def banded(row, count, first, shift):
    wide = jnp.broadcast_to(row, (count, 128))
    return pltpu.roll(wide, (shift + first) % 128, 1, stride=1, stride_axis=0)


def put_main(band, i, out, c, row):
    block = banded(row, 128, 0, 0)
    lane = lax.broadcasted_iota(jnp.int32, (16, 128), 1)
    band[i, out : out + 16, c : c + 128] = jnp.where(lane < 64, block[0:16], 0.0).astype(BF)
    band[i, out + 16 : out + 112, c : c + 128] = block[16:112].astype(BF)
    band[i, out + 112 : out + 128, c : c + 128] = jnp.where(lane >= 64, block[112:128], 0.0).astype(BF)


def edge_band(rows_of, first):
    total = jnp.zeros((16, 128), F32)
    lane = lax.broadcasted_iota(jnp.int32, (16, 128), 1)
    for place, row in rows_of:
        t = lane - 32 * place
        block = banded(row, 16, first, 32 * place + 16)
        ok = (t >= 0) & (t < 16) if first == 0 else (t >= 16) & (t < 32)
        total = total + jnp.where(ok, block, 0.0)
    return total.astype(BF)


def kernel(
    x_hbm, g_hbm, w1_hbm, w2_hbm, quad_hbm, lato_hbm, lono_hbm,
    lo_ref, sg_ref, fin,
    xg, w1_ref, w2_ref, quad_ref, lato_ref, lono_ref, sel,
    ext1, ext2, bsend, brecv, bandf, banda, u_ref, t_ref, slope,
    gs, crecv, xs, xrecv, zrecv, zgroup,
    si, s1, r1, s2, r2, sc, rc, sx, rx, sz, rz, sf, rf, sa, ra, sd, rd, tok,
):
    e, l, x = lax.axis_index("ens"), lax.axis_index("lat"), lax.axis_index("lon")
    yh, core = e // 2, e % 2
    z, yl = l // 2, l % 2
    y = yh * 2 + yl
    me = y * 4 + x
    p, grp = z % 4, z // 4
    up, down = (l + 31) % 32, (l + 1) % 32
    left, right = (x + 3) % 4, (x + 1) % 4
    partner = (yh * 2 + 1 - core, l, x)
    across = ((1 - yh) * 2 + core, z * 2 + 1 - yl, x)

    def xy_peer(s):
        xx, yy = (x + s % 4) % 4, (y + s // 4) % 4
        return yy * 4 + xx, ((yy // 2) * 2 + core, z * 2 + yy % 2, xx)

    def far_first(n):
        def pick(i):
            return (2 + i + (i // 2) * (1 + 2 * (i % 2))) % 4

        return 4 * pick(n // 4) + pick(n % 4)

    def z_device(zz):
        return (e, zz * 2 + yl, x)

    loads = [
        pltpu.make_async_copy(src, dst, si.at[n])
        for n, (src, dst) in enumerate(
            (
                (x_hbm, xg.at[0]), (quad_hbm, quad_ref), (lato_hbm, lato_ref), (lono_hbm, lono_ref),
                (g_hbm, xg.at[1]), (w1_hbm, w1_ref), (w2_hbm, w2_ref),
            )
        )
    ]
    for n in (1, 2, 3, 0, 4, 5, 6):
        loads[n].start()

    barrier = pltpu.get_barrier_semaphore()

    def signal(sem, device):
        pl.semaphore_signal(sem, inc=1, device_id=device, device_id_type=MESH)

    for ll, xx in ((up, x), (down, x), (l, left), (l, right), (up, left), (up, right), (down, left), (down, right)):
        signal(barrier, (e, ll, xx))
    signal(barrier, partner)
    signal(barrier, across)

    at = lax.broadcasted_iota(jnp.int32, (256, 256), 0)
    to = lax.broadcasted_iota(jnp.int32, (256, 256), 1)
    sel[...] = jnp.where(at == jnp.where(to < 128, 2 * to, 2 * to - 255), 1.0, 0.0).astype(BF)

    def turn(f):
        for h in range(2):
            got = dot(xg[f, h * 256 : h * 256 + 256], sel[...], 0, 0).astype(BF)
            for r in range(2):
                ext1[f, 1 + r, :, :, h * 128 : h * 128 + 128] = got[:, r * 128 : r * 128 + 128].reshape(4, 32, 128)

    def rows(ext, f, s, r, n):
        return [
            copy_to(ext.at[f, 1], ext.at[f, 4], s.at[n], r.at[n], (e, up, x)),
            copy_to(ext.at[f, 2], ext.at[f, 0], s.at[n + 1], r.at[n + 1], (e, down, x)),
        ]

    def edges(ext, f, s, r, n):
        return [
            copy_to(ext.at[f, 2, 3, 16:32], ext.at[f, 3, 0, 0:16], s.at[n], r.at[n], (e, down, right)),
            copy_to(ext.at[f, 2, 0, 0:16], ext.at[f, 3, 0, 16:32], s.at[n + 1], r.at[n + 1], (e, down, left)),
            copy_to(ext.at[f, 1, 3, 16:32], ext.at[f, 3, 3, 0:16], s.at[n + 2], r.at[n + 2], (e, up, right)),
            copy_to(ext.at[f, 1, 0, 0:16], ext.at[f, 3, 3, 16:32], s.at[n + 3], r.at[n + 3], (e, up, left)),
            copy_to(ext.at[f, 1:3, 3, 16:32], ext.at[f, 3, 1:3, 0:16], s.at[n + 4], r.at[n + 4], (e, l, right)),
            copy_to(ext.at[f, 1:3, 0, 0:16], ext.at[f, 3, 1:3, 16:32], s.at[n + 5], r.at[n + 5], (e, l, left)),
        ]

    first = [edges(ext1, f, s1, r1, 8 * f) + rows(ext1, f, s1, r1, 8 * f + 6) for f in range(2)]
    first.append(
        [
            copy_to(bsend, brecv.at[1], s1.at[16], r1.at[16], (e, up, x)),
            copy_to(bsend, brecv.at[0], s1.at[17], r1.at[17], (e, down, x)),
        ]
    )
    for n in (1, 2, 3):
        loads[n].wait()
    pad = jnp.zeros((2, 12), jnp.int32)
    lato = jnp.concatenate([lato_ref[:, 0], lato_ref[:, 1], pad])
    lono = jnp.concatenate([lono_ref[:, 0], lono_ref[:, 1], pad])
    quad = jnp.concatenate([quad_ref[:, 0], quad_ref[:, 1], pad.astype(F32)])
    adjoint = tap_rows(quad, lato, lono, -1)
    bsend[...] = adjoint
    loads[0].wait()
    turn(0)
    pl.semaphore_wait(barrier, 10)
    for c in first[2]:
        c.start()
    for c in first[0]:
        c.start()
    loads[4].wait()
    turn(1)
    for c in first[1]:
        c.start()
    for device in ((e, up, x), (e, down, x), (e, l, left), (e, l, right), across):
        signal(tok.at[0], device)

    top, bottom = (l > 0).astype(F32), (l < 31).astype(F32)
    col = ((0, 1, 2, 3), (0, 1, 3, 2))

    def put_bands(band, i, rows):
        for k in range(3):
            for n in range(3):
                put_main(band, i, k * 128, col[i][n] * 128, rows[n](k))
            c = col[i][3] * 128
            places = [(i + n, rows[n](k)) for n in range(3)]
            band[i, k * 128 : k * 128 + 16, c : c + 128] = edge_band(places, 0)
            band[i, k * 128 + 16 : k * 128 + 112, c : c + 128] = jnp.zeros((96, 128), BF)
            band[i, k * 128 + 112 : k * 128 + 128, c : c + 128] = edge_band(places, 112)

    def of(taps, i):
        return lambda k: taps[3 * i + k : 3 * i + k + 1]

    taps = tap_rows(quad, lato, lono, 1)
    fwd = [one_tap(taps, a) for a in range(3)]
    put_bands(bandf, 0, [of(fwd[0] * top, 0), of(fwd[1], 0), of(fwd[2], 0)])
    put_bands(bandf, 1, [of(fwd[0], 1), of(fwd[1], 1), of(fwd[2] * bottom, 1)])
    pl.semaphore_wait(tok.at[0], 5)
    two = (e, l, (x + 2) % 4), ((1 - yh) * 2 + core, l, x), z_device((z + 1) % 16), z_device((z + 15) % 16)
    for device in two:
        signal(tok.at[1], device)
    for c in first[2]:
        c.wait_recv()
    adj = [one_tap(adjoint, a) for a in range(3)]
    put_bands(banda, 0, [of(one_tap(brecv[0], 2) * top, 1), of(adj[1], 0), of(adj[0], 1)])
    put_bands(banda, 1, [of(adj[2], 0), of(adj[1], 1), of(one_tap(brecv[1], 0) * bottom, 0)])

    def spread(band, ext, f, out):
        for i in range(2):
            cells = ext[f, i : i + 4].reshape(512, 256)
            got = dot(band[i], cells, 1, 0).astype(BF)
            for k in range(3):
                out[k, i * 128 : i * 128 + 128] = got[k * 128 : k * 128 + 128]

    def mixed(spreaded, weight, cw):
        total = dot(spreaded[0], weight[0], 1, cw)
        for k in range(1, 3):
            total = total + dot(spreaded[k], weight[k], 1, cw)
        return total

    loads[5].wait()
    loads[6].wait()
    for c in first[0]:
        c.wait_recv()
    spread(bandf, ext1, 0, u_ref)
    hidden = mixed(u_ref, w1_ref, 1)
    root = math.sqrt(2.0 / math.pi)
    square = hidden * hidden
    bend = jnp.tanh(root * hidden * (1.0 + 0.044715 * square))
    act = (0.5 * hidden * (1.0 + bend)).astype(BF)
    slope[...] = 0.5 * (1.0 + bend) + (0.5 * root) * hidden * (1.0 - bend * bend) * (1.0 + (3 * 0.044715) * square)
    ext2[0, 1:3] = act.reshape(2, 4, 32, 256)

    pl.semaphore_wait(tok.at[1], 4)
    for d in (2, 14):
        signal(tok.at[2], z_device((z + d) % 16))
    for c in first[1]:
        c.wait_recv()
    spread(banda, ext1, 1, t_ref)

    def put_grad(ch, row, value):
        value = value.astype(BF)
        gs[ch, 0, row : row + 256] = value[:, :128]
        gs[ch, 1, row : row + 256] = value[:, 128:]

    cores = [
        copy_to(gs.at[ch, 1 - core], crecv.at[ch], sc.at[ch], rc.at[ch], partner) for ch in range(2)
    ]
    for k in range(3):
        put_grad(0, k * 256, dot(t_ref[k], act, 0, 0))
    cores[0].start()
    act_grad = mixed(t_ref, w2_ref, 0).astype(BF).astype(F32)
    hid_grad = (act_grad * slope[...]).astype(BF)
    ext2[1, 1:3] = hid_grad.reshape(2, 4, 32, 256)
    for k in range(3):
        put_grad(1, k * 256, dot(hid_grad, u_ref[k], 0, 0))
    cores[1].start()
    pl.semaphore_wait(tok.at[2], 2)
    for d in (4, 12):
        signal(tok.at[3], z_device((z + d) % 16))

    def piece(ch, s):
        peer, device = xy_peer(s)
        rows = pl.ds(pl.multiple_of(peer * PIECE, 16), PIECE)
        return copy_to(xs.at[ch, rows], xrecv.at[ch, s - 1], sx.at[ch, s - 1], rx.at[ch, s - 1], device)

    for ch in range(2):
        cores[ch].wait_recv()
        xs[ch] = (gs[ch, core].astype(F32) + crecv[ch].astype(F32)).astype(BF)

        def send_piece(s, c, ch=ch):
            piece(ch, far_first(s)).start()
            return c

        lax.fori_loop(0, 15, send_piece, 0)

    mine = pl.ds(pl.multiple_of(me * PIECE, 16), PIECE)

    def near(ch, s):
        return copy_to(zrecv.at[ch, p], zrecv.at[ch, p], sz.at[ch, s - 1], rz.at[ch, p], z_device(grp * 4 + (p + s) % 4))

    def near_in(ch, s):
        q = (p + s) % 4
        return copy_to(zrecv.at[ch, q], zrecv.at[ch, q], sz.at[ch, s - 1], rz.at[ch, q], z_device(grp * 4 + q))

    for ch in range(2):

        def add_piece(s, total, ch=ch):
            piece(ch, s).wait_recv()
            return total + xrecv[ch, s - 1].astype(F32)

        zrecv[ch, p] = lax.fori_loop(1, 16, add_piece, xs[ch, mine].astype(F32)).astype(BF)
        for s in range(1, 4):
            near(ch, s).start()

    second = [c for f in range(2) for c in rows(ext2, f, s2, r2, 8 * f) + edges(ext2, f, s2, r2, 8 * f + 2)]

    for c in second:
        c.start()

    def far(ch, n, group, member):
        return copy_to(
            zgroup.at[ch, grp], zgroup.at[ch, grp], sf.at[ch, n], rf.at[ch, grp], z_device(group * 4 + member)
        )

    before, after, opposite = (grp + 3) % 4, (grp + 1) % 4, (grp + 2) % 4
    to_left = [(opposite, 2), (opposite, 3), (before, 0), (before, 1), (before, 2), (before, 3)]
    to_right = [(opposite, 1), (opposite, 0), (after, 3), (after, 2), (after, 1), (after, 0)]

    def all_four(ref):
        total = ref[0].astype(F32)
        for q in range(1, 4):
            total = total + ref[q].astype(F32)
        return total.astype(BF)

    pl.semaphore_wait(tok.at[3], 2)
    for ch in range(2):
        for s in range(1, 4):
            near_in(ch, s).wait_recv()
        zgroup[ch, grp] = all_four(zrecv.at[ch])

        @pl.when(p == 0)
        def _(ch=ch):
            for n in range(6):
                far(ch, n, *to_left[n]).start()

        @pl.when(p == 3)
        def _(ch=ch):
            for n in range(6):
                far(ch, n, *to_right[n]).start()

    def spread_piece(ch, s):
        cells = fin.at[ch, core, mine]
        return copy_to(cells, cells, sa.at[ch, s - 1], ra.at[ch, s - 1], xy_peer(s)[1])

    for ch in range(2):
        for s in range(1, 4):
            q = (grp + s) % 4
            cells = zgroup.at[ch, q]
            copy_to(cells, cells, sf.at[ch, 0], rf.at[ch, q], z_device(q * 4)).wait_recv()
        fin[ch, core, mine] = all_four(zgroup.at[ch])

        def send_back(s, c, ch=ch):
            spread_piece(ch, far_first(s)).start()
            return c

        lax.fori_loop(0, 15, send_back, 0)

    swaps = [copy_to(fin.at[ch, core], fin.at[ch, core], sd.at[ch], rd.at[ch], partner) for ch in range(2)]
    for ch in range(2):

        def wait_back(s, c, ch=ch):
            spread_piece(ch, s).wait()
            return c

        lax.fori_loop(1, 16, wait_back, 0)
        swaps[ch].start()

    def turned_back(cells, out):
        for h in range(2):
            lanes = slice(h * 128, h * 128 + 128)
            both = jnp.concatenate([cells[0:128, lanes], cells[128:256, lanes]], axis=1)
            out[h * 256 : h * 256 + 256] = dot(sel[...], both, 1, 1).astype(BF)

    for c in second:
        c.wait_recv()
    spread(bandf, ext2, 0, u_ref)
    turned_back(mixed(u_ref, w2_ref, 1).astype(BF), lo_ref)
    spread(banda, ext2, 1, t_ref)
    turned_back(mixed(t_ref, w1_ref, 0).astype(BF), sg_ref)

    for c in first[0] + first[1] + first[2] + second + cores:
        c.wait_send()
    for ch in range(2):

        def wait_sent(s, c, ch=ch):
            piece(ch, s).wait_send()
            return c

        lax.fori_loop(1, 16, wait_sent, 0)
        for s in range(1, 4):
            near(ch, s).wait_send()

        @pl.when(p == 0)
        def _(ch=ch):
            for n in range(6):
                far(ch, n, *to_left[n]).wait_send()

        @pl.when(p == 3)
        def _(ch=ch):
            for n in range(6):
                far(ch, n, *to_right[n]).wait_send()
    for c in swaps:
        c.wait()


def finish(lo_ref, sg_ref, fin, lo_hbm, sg_hbm, d1_hbm, d2_hbm, d_ref, sems):
    stores = [
        pltpu.make_async_copy(lo_ref, lo_hbm, sems.at[6]),
        pltpu.make_async_copy(sg_ref, sg_hbm, sems.at[7]),
    ]
    scale = 1.0 / math.sqrt(4 * 64 * 512)
    for n in range(2):
        for k in range(3):
            for h in range(2):
                rows = slice(k * 256, k * 256 + 256)
                d_ref[n, k, :, h * 128 : h * 128 + 128] = fin[n, h, rows].astype(F32) * scale
            stores.append(pltpu.make_async_copy(d_ref.at[n, k], (d2_hbm, d1_hbm)[n].at[k], sems.at[3 * n + k]))
            stores[-1].start()
    stores[0].start()
    stores[1].start()
    for c in stores:
        c.wait()


def body(state_field, first_weight, second_weight, quadrature, lat_offsets, lon_offsets, cotangent):
    vmem = pl.BlockSpec(memory_space=pltpu.VMEM)
    anywhere = pl.BlockSpec(memory_space=pl.ANY)
    dma = pltpu.SemaphoreType.DMA
    lo, sg, fin = pl.pallas_call(
        kernel,
        out_shape=(
            pltpu.VMEM((512, 128), BF),
            pltpu.VMEM((512, 128), BF),
            pltpu.VMEM((2, 2, 768, 128), BF),
        ),
        in_specs=[anywhere] * 7,
        out_specs=[vmem] * 3,
        scratch_shapes=[
            pltpu.VMEM((2, 512, 128), BF),
            pltpu.VMEM((3, 256, 256), BF),
            pltpu.VMEM((3, 256, 256), BF),
            pltpu.VMEM((3, 2, 12), F32),
            pltpu.VMEM((3, 2, 12), jnp.int32),
            pltpu.VMEM((3, 2, 12), jnp.int32),
            pltpu.VMEM((256, 256), BF),
            pltpu.VMEM((2, 5, 4, 32, 256), BF),
            pltpu.VMEM((2, 5, 4, 32, 256), BF),
            pltpu.VMEM((8, 128), F32),
            pltpu.VMEM((2, 8, 128), F32),
            pltpu.VMEM((2, 384, 512), BF),
            pltpu.VMEM((2, 384, 512), BF),
            pltpu.VMEM((3, 256, 256), BF),
            pltpu.VMEM((3, 256, 256), BF),
            pltpu.VMEM((256, 256), F32),
            pltpu.VMEM((2, 2, 768, 128), BF),
            pltpu.VMEM((2, 768, 128), BF),
            pltpu.VMEM((2, 768, 128), BF),
            pltpu.VMEM((2, 15, PIECE, 128), BF),
            pltpu.VMEM((2, 4, PIECE, 128), BF),
            pltpu.VMEM((2, 4, PIECE, 128), BF),
            dma((7,)),
            dma((18,)), dma((18,)),
            dma((16,)), dma((16,)),
            dma((2,)), dma((2,)),
            dma((2, 15)), dma((2, 15)),
            dma((2, 3)), dma((2, 4)),
            dma((2, 6)), dma((2, 4)),
            dma((2, 15)), dma((2, 15)),
            dma((2,)), dma((2,)),
            pltpu.SemaphoreType.REGULAR((4,)),
        ],
        compiler_params=pltpu.CompilerParams(collective_id=0, has_side_effects=True, vmem_limit_bytes=60 * 2**20),
        cost_estimate=pl.CostEstimate(flops=1_500_000_000, bytes_accessed=4_000_000, transcendentals=65536),
        name="conv_pair",
    )(
        state_field.reshape(512, 128),
        cotangent.reshape(512, 128),
        first_weight,
        second_weight,
        *(jnp.transpose(t, (1, 0, 2)) for t in (quadrature, lat_offsets, lon_offsets)),
    )
    lo, sg, d1, d2 = pl.pallas_call(
        finish,
        out_shape=(
            jax.ShapeDtypeStruct((512, 128), BF),
            jax.ShapeDtypeStruct((512, 128), BF),
            jax.ShapeDtypeStruct((3, 256, 256), F32),
            jax.ShapeDtypeStruct((3, 256, 256), F32),
        ),
        in_specs=[vmem] * 3,
        out_specs=[anywhere] * 4,
        scratch_shapes=[pltpu.VMEM((2, 3, 256, 256), F32), dma((8,))],
        compiler_params=pltpu.CompilerParams(vmem_limit_bytes=4 * 2**20),
        name="put_out",
    )(lo, sg, fin)
    return lo.reshape(1, 256, 2, 128), sg.reshape(1, 256, 2, 128), d1, d2


def solution(mesh):
    in_specs = (
        P("ens", None, "lat", "lon"),
        P(),
        P(),
        P("lat", None, None),
        P("lat", None, None),
        P("lat", None, None),
        P("ens", None, "lat", "lon"),
    )
    out_specs = (P("ens", None, "lat", "lon"), P("ens", None, "lat", "lon"), P(), P())
    return jax.shard_map(body, mesh=mesh, in_specs=in_specs, out_specs=out_specs, check_vma=False)
```
